512 devices in a mesh: ctx: 64 (over z, x, core), dp: 8 (over y).
Axes of the slice: x: 4, y: 8, z: 8, core: 2. Of those that a mesh axis runs over, the one named last changes fastest.
Arguments:
- tokens: bfloat16 [8, 8192, 5376], P('dp', 'ctx'), may hold values from -6 to 6
- norm_gain: bfloat16 [5376], replicated, may hold values from 0.5 to 1.5
- queries: bfloat16 [8, 8192, 128], P('dp', 'ctx'), may hold values from -6 to 6
- values: bfloat16 [8, 8192, 128], P('dp', 'ctx'), may hold values from -6 to 6
- upstream: bfloat16 [8, 8192, 128], P('dp', 'ctx'), may hold values from -6 to 6
- segments: int32 [8, 8192], P('dp', 'ctx'), may hold values from 0 to 7, never falling along the last dimension, each value on 1 to 2048 neighbouring positions
- key_weight: bfloat16 [5376, 128], P('ctx', 'dp'), may hold values from -0.078125 to 0.078125
- key_gain: float32 [128], replicated, may hold values from 0.25 to 1.75
- direction: float32 [5376, 128], P('ctx', 'dp'), may hold values from -6 to 6
- stored_basis: float32 [6, 5376, 128], P(None, 'ctx', 'dp'), may hold values from -103.68593 to 103.68593
Outputs:
- coefficients: float32 [7], replicated
- beta: float32 [], replicated
- next_vector: float32 [5376, 128], P('ctx', 'dp')
The draws below stay inside these ranges and needn't reach their ends.
Inputs may be any that keep to these rules, and one draw needn't show every extreme that they name: `segments`: within each sequence the document ids never fall; each document holds 1 to 2048 tokens, and one of them exactly that many.
All inputs are finite; a program needn't handle non-finite values.
Results may differ from the reference program's by a relative error of at most 0.0035.
The reference program's roundings to bfloat16 on the way (of `normed`, `tangent` and `cot_tan`) count: a program that leaves them out, or rounds other values in their place, can miss the bound.
Values may be sent and summed in bfloat16 or wider, within the bound.
A program may use at most 64 MiB of HBM per device.

```python
import math
import jax
import jax.numpy as jnp
import numpy as np
from jax import lax

D = 5376
HD = 128
WINDOW = 1024
TOK_DEV = 128
NVEC = 6
LENGTH = 8192
SEQS = 8
N_CTX = 64


def levels(stream_key, extent, cuts, least, largest):
    factor_of = 1.0
    for dim, parts in cuts:
        steps = jax.random.uniform(jax.random.fold_in(jax.random.fold_in(stream_key, 6), dim), (parts,), jnp.float32, least / len(cuts), largest / len(cuts))
        factor_of = factor_of * jnp.repeat(jnp.exp(steps), extent[dim] // parts).reshape((-1,) + (1,) * (len(extent) - 1 - dim))
    return factor_of


def split_up(amount, total, most, lean):
    weights = [(1 << 20) // math.isqrt(grade ** lean) + 1 for grade in range(2, amount + 1)]
    spare, holding = total - most - (amount - 1), [1] * (amount - 1)
    while spare > 0:
        free = [i for i in range(amount - 1) if holding[i] < most]
        mass, left = sum([weights[i] for i in free]), spare
        for i in free:
            addition = min(most - holding[i], max(1, left * weights[i] // mass), spare)
            holding[i] = holding[i] + addition
            spare = spare - addition
    return np.array([most] + holding)


def ragged_sizes(rng, number_of, total, limit, skew):
    if number_of == 2:
        one = jax.random.randint(rng, (), max(1, total - limit), min(limit, total - 1) + 1)
        return jnp.stack([one, total - one])
    tallies = jnp.asarray(split_up(number_of, total, limit, skew), jnp.int32)
    couples = (number_of - 1) // 2
    giver, sink = tallies[1:1 + 2 * couples:2], tallies[2:2 + 2 * couples:2]
    room = jnp.minimum(giver - 1, limit - sink)
    moved = jax.random.randint(jax.random.fold_in(rng, 1), (couples,), 0, 1 << 20) % (room + 1)
    tallies = tallies.at[1:1 + 2 * couples:2].set(giver - moved).at[2:2 + 2 * couples:2].set(sink + moved)
    return tallies[jax.random.permutation(jax.random.fold_in(rng, 2), number_of)]


def noise(own_key, dims, spread, limit, shards=(), kind=jnp.bfloat16):
    loudness = levels(own_key, dims, shards, -0.22, 0.18) if shards else 1.0
    result = jax.random.normal(own_key, dims, jnp.float32) * spread * loudness
    return jnp.minimum(jnp.maximum(result, -limit), limit).astype(kind)


def setup_inputs(seed: int = 0) -> dict:
    streams_of = jax.random.split(jax.random.key(seed), 11)
    tokens = noise(streams_of[0], (SEQS, LENGTH, D), 1.0, 6.0, ((0, 8), (1, 64)))
    norm_gain = jnp.clip(1.0 + 0.1 * jax.random.normal(streams_of[1], (D,), jnp.float32), 0.5, 1.5).astype(jnp.bfloat16)
    queries = noise(streams_of[2], (SEQS, LENGTH, HD), 1.0, 6.0, ((0, 8), (1, 64)))
    values = noise(streams_of[3], (SEQS, LENGTH, HD), 1.0, 6.0, ((0, 8), (1, 64)))
    upstream = noise(streams_of[4], (SEQS, LENGTH, HD), 1.0, 6.0, ((0, 8), (1, 64)))
    segments = jax.vmap(lambda own: jnp.searchsorted(jnp.cumsum(ragged_sizes(own, TOK_DEV * N_CTX // WINDOW, LENGTH, 2 * WINDOW, 1)), jnp.arange(LENGTH), side="right"))(jax.random.split(streams_of[5], SEQS)).reshape((SEQS, LENGTH)).astype(jnp.int32)
    key_weight = noise(streams_of[6], (D, HD), D ** -0.5, 0.078125, ((0, 64), (1, 8)))
    key_gain = jnp.clip(1.0 + 0.15 * jax.random.normal(streams_of[7], (HD,), jnp.float32), 0.25, 1.75)
    direction = noise(streams_of[8], (D, HD), 1.0, 6.0, ((0, 64), (1, 8)), jnp.float32)
    stored_basis = noise(streams_of[9], (NVEC, D, HD), (0.6 * (D * HD) ** 0.25), 103.68593, ((1, 64), (2, 8)), jnp.float32)
    return dict(tokens=tokens, norm_gain=norm_gain, queries=queries, values=values, upstream=upstream, segments=segments, key_weight=key_weight, key_gain=key_gain, direction=direction, stored_basis=stored_basis)


SCORE_SCALE = 168.0 ** (-0.5)
EPSILON = 1e-06

def normalize(activations, gain_vector):
    floats = activations.astype(jnp.float32)
    scaled = floats * lax.rsqrt(lax.optimization_barrier(jnp.mean(floats * floats, axis=-1, keepdims=True)) + EPSILON)
    return (scaled * gain_vector.astype(jnp.float32)).astype(jnp.bfloat16)

def rotate(vectors, places):
    half_width = vectors.shape[-1] // 2
    freqs = 10000.0 ** (-jnp.arange(half_width, dtype=jnp.float32) / half_width)
    angles = places.astype(jnp.float32)[:, None] * freqs[None, :]
    cosine = jnp.cos(angles)
    sine = jnp.sin(angles)
    first_half = vectors[:, :half_width]
    second_half = vectors[:, half_width:]
    return jnp.concatenate([first_half * cosine - second_half * sine, second_half * cosine + first_half * sine], axis=1)

def key_map(linear, places, scales):
    normed_keys = linear * lax.rsqrt(lax.optimization_barrier(jnp.mean(linear * linear, axis=-1, keepdims=True)) + EPSILON) * scales
    return rotate(normed_keys, places)

def key_cotangent(linear, cotangent, places, scales):
    return jax.vjp(lambda inner: key_map(inner, places, scales), linear)[1](cotangent)[0]

def band_mask(query_pos, query_doc, key_pos, key_doc):
    near = (key_pos[None, :] <= query_pos[:, None]) & (key_pos[None, :] > query_pos[:, None] - WINDOW)
    return near & (key_pos[None, :] >= 0) & (key_doc[None, :] == query_doc[:, None])

def band_loss(key_cat, query_rows, value_cat, upstream_rows, allowed):
    scores = jnp.dot(query_rows, key_cat.T, precision=lax.Precision.HIGHEST) * SCORE_SCALE
    expos = jnp.where(allowed, jnp.exp(scores), 0.0)
    weights = expos / lax.optimization_barrier(jnp.sum(expos, axis=-1, keepdims=True))
    output = jnp.dot(weights, value_cat, precision=lax.Precision.HIGHEST)
    return jnp.sum(upstream_rows * output)

def band_grads(key_cat, key_tan, query_rows, value_cat, upstream_rows, allowed):

    def gradient(keys_in):
        return jax.grad(band_loss)(keys_in, query_rows, value_cat, upstream_rows, allowed)
    return jax.jvp(gradient, (key_cat,), (key_tan,))

def reference(tokens, norm_gain, queries, values, upstream, segments, key_weight, key_gain, direction, stored_basis):
    reach = (WINDOW + TOK_DEV - 1) // TOK_DEV
    margin = reach * TOK_DEV
    span = margin + TOK_DEV
    tangent = (direction * D ** (-0.5)).astype(jnp.bfloat16)

    def one_sequence(running, items):
        rows_in, query_in, value_in, upper_in, doc_in = items
        normed = normalize(rows_in, norm_gain)
        key_lin = jnp.dot(normed, key_weight, preferred_element_type=jnp.float32)
        tangent_lin = jnp.dot(normed, tangent, preferred_element_type=jnp.float32)
        places = jnp.arange(LENGTH, dtype=jnp.int32)
        keyed, keyed_tan = jax.jvp(lambda inner: key_map(inner, places, key_gain), (key_lin,), (tangent_lin,))
        padding = jnp.zeros((margin, HD), jnp.float32)
        key_pad = jnp.concatenate([padding, keyed], axis=0)
        tan_pad = jnp.concatenate([padding, keyed_tan], axis=0)
        value_pad = jnp.concatenate([padding, value_in.astype(jnp.float32)], axis=0)
        doc_pad = jnp.concatenate([jnp.zeros((margin,), jnp.int32), doc_in], axis=0)
        place_pad = jnp.arange(LENGTH + margin, dtype=jnp.int32) - margin
        query_float = query_in.astype(jnp.float32)
        upper_float = upper_in.astype(jnp.float32)

        def one_block(carried, begin):
            key_cat = lax.dynamic_slice_in_dim(key_pad, begin, span, 0)
            tan_cat = lax.dynamic_slice_in_dim(tan_pad, begin, span, 0)
            value_cat = lax.dynamic_slice_in_dim(value_pad, begin, span, 0)
            key_doc = lax.dynamic_slice_in_dim(doc_pad, begin, span, 0)
            key_pos = lax.dynamic_slice_in_dim(place_pad, begin, span, 0)
            query_rows = lax.dynamic_slice_in_dim(query_float, begin, TOK_DEV, 0)
            upper_rows = lax.dynamic_slice_in_dim(upper_float, begin, TOK_DEV, 0)
            query_doc = lax.dynamic_slice_in_dim(doc_in, begin, TOK_DEV, 0)
            query_pos = lax.dynamic_slice_in_dim(places, begin, TOK_DEV, 0)
            allowed = band_mask(query_pos, query_doc, key_pos, key_doc)
            grads, grads_tan = band_grads(key_cat, tan_cat, query_rows, value_cat, upper_rows, allowed)
            sum_grad = lax.dynamic_slice_in_dim(carried[0], begin, span, 0) + grads
            sum_tan = lax.dynamic_slice_in_dim(carried[1], begin, span, 0) + grads_tan
            return ((lax.dynamic_update_slice_in_dim(carried[0], sum_grad, begin, 0), lax.dynamic_update_slice_in_dim(carried[1], sum_tan, begin, 0)), None)
        begins = jnp.arange(LENGTH // TOK_DEV, dtype=jnp.int32) * TOK_DEV
        empty = jnp.zeros((LENGTH + margin, HD), jnp.float32)
        (grad_pad, tan_grad_pad), _ = lax.scan(one_block, (empty, empty), begins)
        grad_keys = grad_pad[margin:]
        grad_tan = tan_grad_pad[margin:]
        _, cot_tan = jax.jvp(lambda inner, cotangent: key_cotangent(inner, cotangent, places, key_gain), (key_lin, grad_keys), (tangent_lin, grad_tan))
        rounded = cot_tan.astype(jnp.bfloat16)
        term = lax.dot_general(normed, rounded, (((0,), (0,)), ((), ())), preferred_element_type=jnp.float32)
        return (running + term, None)
    summed, _ = lax.scan(one_sequence, jnp.zeros((D, HD), jnp.float32), (tokens, queries, values, upstream, segments))
    product = summed * D ** (-0.5)
    stacked = jnp.concatenate([stored_basis, direction[None]], axis=0)
    entries = D * HD
    coefficients = jnp.einsum('kdh,dh->k', stacked, product, precision=lax.Precision.HIGHEST) / entries
    residual = product - jnp.einsum('k,kdh->dh', coefficients, stacked, precision=lax.Precision.HIGHEST)
    beta = jnp.sqrt(jnp.sum(residual * residual) / entries + EPSILON)
    return (coefficients, beta, residual / beta)
```

```python
import jax
import jax.numpy as jnp
import numpy as np
from jax import lax
from jax.experimental import pallas as pl
from jax.experimental.pallas import tpu as pltpu
from jax.sharding import PartitionSpec as P

D = 5376
HD = 128
WINDOW = 1024
HALF = D // 2
ROWS = 84
SCORE_SCALE = 168.0 ** (-0.5)
EPSILON = 1e-06
ENTRIES = D * HD
GROUP = 768
LOW = -1e30
MESH = pl.DeviceIdType.MESH
F32 = jnp.float32
BF16 = jnp.bfloat16
FREQS = np.tile(10000.0 ** (-np.arange(64) / 64.0), 2)[None].astype(np.float32)


def dot_nt(a, b):
    return lax.dot_general(a, b, (((1,), (1,)), ((), ())), preferred_element_type=F32)


def dot_nn(a, b):
    return lax.dot_general(a, b, (((1,), (0,)), ((), ())), preferred_element_type=F32)


def split(a):
    high = a.astype(BF16)
    return high, (a - high.astype(F32)).astype(BF16)


def ring_step(t):
    odd = t % 2
    return odd * (8 - (t + 1) // 2) + (1 - odd) * ((t + 2) // 2)


def far_step(t):
    return ring_step(6 - t)


def kernel(
    tok,
    gain,
    q_in,
    v_in,
    u_in,
    seg_in,
    wt,
    kg,
    freq_in,
    bas,
    out,
    aux,
    g1,
    wb,
    nb,
    ns,
    qu,
    segb,
    kl,
    klr,
    ev,
    sv,
    gv,
    rst,
    cott,
    acc,
    tb,
    rx,
    py,
    ry,
    pz,
    rz,
    ar,
    cs,
    g1_s,
    g1_r,
    qu_s,
    qu_r,
    sg_s,
    sg_r,
    y_s,
    y_r,
    x_s,
    x_r,
    one_s,
    one_r,
    st_s,
    st_r,
    rx_s,
    rx_r,
    ry_s,
    ry_r,
    rz_s,
    rz_r,
    ar_s,
    ar_r,
):
    ctx = lax.axis_index("ctx")
    y = lax.axis_index("dp")
    z = ctx // 8
    x = (ctx // 2) % 4
    k = ctx % 2
    half = z // 4
    zz = z % 4

    def at_z(zi, ki):
        return ((zi * 4 + x) * 2 + ki, y)

    def at_x(xi):
        return ((z * 4 + xi) * 2 + k, y)

    def at_y(yi):
        return (ctx, yi)

    def at_ctx(ci):
        return (ci % 64, y)

    other = ((z * 4 + x) * 2 + (1 - k), y)

    def rdma(src, dst, send, recv, device):
        return pltpu.make_async_remote_copy(
            src_ref=src,
            dst_ref=dst,
            send_sem=send,
            recv_sem=recv,
            device_id=device,
            device_id_type=MESH,
        )

    barrier = pltpu.get_barrier_semaphore()

    def greet(device):
        pl.semaphore_signal(barrier, inc=1, device_id=device, device_id_type=MESH)

    for d in range(1, 9):
        greet(at_ctx(ctx + d))
        greet(at_ctx(ctx + 64 - d))
    for dz in range(2, 7):
        greet(at_z((z + dz) % 8, 0))
        greet(at_z((z + dz) % 8, 1))
    for dz in (1, 7):
        greet(at_z((z + dz) % 8, 1 - k))
    for dy in range(1, 8):
        greet(at_y((y + dy) % 8))

    qu[0, 0] = q_in[...]
    qu[0, 1] = u_in[...]
    segb[0] = jnp.broadcast_to(seg_in[...], (8, 128))
    pl.semaphore_wait(barrier, 35)

    own_slot = zz * 2 + k

    def g1_copy(zi, slot):
        return rdma(wt, g1.at[slot], g1_s.at[zi], g1_r.at[slot], at_z(zi, half))

    def g1_send(t, _):
        zi = (z + t) % 8

        @pl.when(jnp.logical_or(zi != z, half != k))
        def _():
            g1_copy(zi, own_slot).start()

        return 0

    lax.fori_loop(0, 8, g1_send, 0)

    @pl.when(half == k)
    def _():
        g1[own_slot] = wt[...]

    def qu_copy(j):
        return rdma(qu.at[0], qu.at[j], qu_s.at[j - 1], qu_r.at[j - 1], at_ctx(ctx + 64 - j))

    def sg_copy(j):
        return rdma(segb.at[0], segb.at[j], sg_s.at[j - 1], sg_r.at[j - 1], at_ctx(ctx + 64 - j))

    def qu_send(j, _):
        qu_copy(j).start()
        sg_copy(j).start()
        return 0

    lax.fori_loop(1, 9, qu_send, 0)

    lane128 = lax.broadcasted_iota(jnp.int32, (1, 128), 1)
    gain_row = gain[...].astype(F32)

    def norm_chunk(r):
        rows = pl.ds(pl.multiple_of(r * 16, 16), 16)
        floats = tok[rows, :].astype(F32)
        scale = lax.rsqrt(jnp.mean(floats * floats, axis=-1, keepdims=True) + EPSILON)
        normed = floats * scale * gain_row
        for hh in range(2):
            for xi in range(4):
                tiles = [jnp.zeros((16, 128), F32) for _ in range(6)]
                for zi in range(4):
                    start = hh * HALF + zi * 672 + xi * 168
                    first = min(start // 128, D // 128 - 3)
                    shift = start - first * 128
                    goal, lead = (168 * zi) // 128, (168 * zi) % 128
                    slab = normed[:, first * 128 : first * 128 + 384]
                    moved = pltpu.roll(slab, (lead - shift) % 384, 1) if lead != shift else slab
                    for m in range(3):
                        low, high = lead - 128 * m, lead + 168 - 128 * m
                        if high <= 0 or low >= 128:
                            continue
                        part = moved[:, 128 * m : 128 * m + 128]
                        if low > 0 or high < 128:
                            inside = jnp.logical_and(lane128 >= low, lane128 < high)
                            part = jnp.where(inside, part, 0.0)
                        tiles[goal + m] = tiles[goal + m] + part
                group = jnp.concatenate(tiles, axis=1).astype(BF16)

                @pl.when(k == hh)
                def _():
                    nb[xi, pl.ds(pl.multiple_of(k * 128 + r * 16, 16), 16), :] = group

                @pl.when(k != hh)
                def _():
                    ns[xi, rows, :] = group

    norm_chunk(7)

    def g1_wait(slot, _):
        zi = half * 0 + k * 4 + slot // 2
        mine = jnp.logical_and(zi == z, slot % 2 == k)

        @pl.when(jnp.logical_not(mine))
        def _():
            g1_copy(z, slot).wait_recv()

        return 0

    lax.fori_loop(0, 8, g1_wait, 0)
    tiles = [jnp.zeros((32, 128), F32) for _ in range(6)]
    for slot in range(8):
        piece = g1[slot].astype(F32).reshape(32, 128)
        goal, lead = (ROWS * slot) // 128, (ROWS * slot) % 128
        moved = pltpu.roll(piece, lead, 1) if lead else piece
        tiles[goal] = tiles[goal] + jnp.where(lane128 >= lead, moved, 0.0)
        if lead + ROWS > 128:
            tiles[goal + 1] = tiles[goal + 1] + jnp.where(lane128 < lead, moved, 0.0)
    block = jnp.concatenate(tiles, axis=1).astype(BF16)
    my_cols = pl.ds(pl.multiple_of(y * 16, 16), 16)
    wb[x, 0, my_cols, :] = block[0:16]
    wb[x, 1, my_cols, :] = block[16:32]

    def piece_at(xi, yi):
        return wb.at[xi, :, pl.ds(pl.multiple_of(yi * 16, 16), 16), :]

    def y_copy(src_y, dst_y, t):
        return rdma(piece_at(x, src_y), piece_at(x, src_y), y_s.at[t], y_r.at[src_y], at_y(dst_y))

    def x_copy(src_x, yi, dst_x, t):
        return rdma(
            piece_at(src_x, yi), piece_at(src_x, yi), x_s.at[t, yi], x_r.at[src_x, yi], at_x(dst_x)
        )

    def y_send(t, _):
        y_copy(y, (y + far_step(t)) % 8, t).start()
        return 0

    lax.fori_loop(0, 7, y_send, 0)

    def x_send(yi):
        for t, dx in enumerate((2, 1, 3)):
            x_copy(x, yi, (x + dx) % 4, t).start()

    x_send(y)

    def y_forward(t, _):
        norm_chunk(t)
        src = (y + ring_step(t)) % 8
        y_copy(src, y, 0).wait_recv()
        x_send(src)
        return 0

    lax.fori_loop(0, 7, y_forward, 0)

    swap = rdma(ns, nb.at[:, pl.ds(pl.multiple_of(k * 128, 128), 128), :], one_s.at[0], one_r.at[0], other)
    swap.start()

    lane = lax.broadcasted_iota(jnp.int32, (128, 128), 1)
    sub = lax.broadcasted_iota(jnp.int32, (128, 128), 0)
    angle = (ctx * 128 + sub).astype(F32) * freq_in[...]
    cs[0] = jnp.cos(angle)
    cs[1] = jnp.sin(angle) * jnp.where(lane < 64, -1.0, 1.0)
    key_doc = jnp.transpose(jnp.broadcast_to(segb[0, 0:1].astype(F32), (128, 128)))

    lane8 = lax.broadcasted_iota(jnp.int32, (8, 128), 1)
    sub8 = lax.broadcasted_iota(jnp.int32, (8, 128), 0)
    gram = jnp.zeros((8, 128), F32)
    for a in range(7):
        for b in range(a, 7):
            dotted = jnp.sum(jnp.sum(bas[a] * bas[b], axis=0, keepdims=True), axis=1, keepdims=True)
            spot = jnp.logical_and(sub8 == a, lane8 == b)
            if a != b:
                spot = jnp.logical_or(spot, jnp.logical_and(sub8 == b, lane8 == a))
            gram = jnp.where(spot, dotted, gram)

    swap.wait_recv()
    for dx in range(4):
        xi = (x + dx) % 4
        if dx:

            def x_wait(yi, _):
                x_copy(xi, yi, x, 0).wait_recv()
                return 0

            lax.fori_loop(0, 8, x_wait, 0)
        part = dot_nt(nb[xi], wb[xi].reshape(256, GROUP))
        if dx:
            kl[...] += part
        else:
            kl[...] = part
    mine = pl.ds(pl.multiple_of(k * 128, 128), 128)
    theirs = pl.ds(pl.multiple_of((1 - k) * 128, 128), 128)
    kl_swap = rdma(kl.at[theirs], klr, one_s.at[1], one_r.at[1], other)
    kl_swap.start()

    def qu_wait(j, _):
        qu_copy(j).wait_recv()
        sg_copy(j).wait_recv()
        return 0

    lax.fori_loop(1, 9, qu_wait, 0)
    kl_swap.wait_recv()
    both = kl[mine, :] + klr[...]
    lin, tan = both[:, 0:128], both[:, 128:256]
    cosine, sine = cs[0], cs[1]
    key_gain = kg[...]

    def rope(vec):
        return vec * cosine + pltpu.roll(vec, 64, 1) * sine

    def rope_back(vec):
        return vec * cosine - pltpu.roll(vec, 64, 1) * sine

    def mean(vec):
        return jnp.mean(vec, axis=-1, keepdims=True)

    inv = lax.rsqrt(mean(lin * lin) + EPSILON)
    inv3 = inv * inv * inv
    inv_tan = -inv3 * mean(lin * tan)
    keyed = rope(lin * inv * key_gain) * SCORE_SCALE
    keyed_tan = rope((tan * inv + lin * inv_tan) * key_gain) * SCORE_SCALE
    k_high, k_low = split(keyed)
    t_high, t_low = split(keyed_tan)
    stacked_keys = jnp.concatenate([k_high, k_low, t_high, t_low], axis=0)
    value_rows = v_in[...]

    def score(j, _):
        raw = dot_nt(stacked_keys, qu[j, 0])
        s = raw[0:128] + raw[128:256]
        st = raw[256:384] + raw[384:512]
        g = dot_nt(value_rows, qu[j, 1])
        gap = 128 * j + lane - sub
        near = jnp.logical_and(gap >= 0, gap < WINDOW)
        same = key_doc == segb[j, 0:1].astype(F32)
        allowed = jnp.logical_and(jnp.logical_and(near, same), ctx + j < 64)
        top = jnp.max(jnp.where(allowed, s, LOW), axis=0, keepdims=True)
        e = jnp.where(allowed, jnp.exp(s - top), 0.0)
        est = e * st
        rows = [top] + [jnp.sum(m, axis=0, keepdims=True) for m in (e, e * g, est, est * g)]
        rst[8, j] = jnp.concatenate(rows + [jnp.zeros((3, 128), F32)], axis=0)
        ev[j] = e
        sv[j] = st
        gv[j] = g
        return 0

    lax.fori_loop(0, 9, score, 0)

    def st_copies():
        copies = []
        for d in range(1, 9):
            n = 9 - d
            copies.append(
                rdma(
                    rst.at[8, pl.ds(d, n)],
                    rst.at[8 + d, pl.ds(0, n)],
                    st_s.at[d - 1],
                    st_r.at[d - 1],
                    at_ctx(ctx + d),
                )
            )
            copies.append(
                rdma(
                    rst.at[8, pl.ds(0, n)],
                    rst.at[8 - d, pl.ds(d, n)],
                    st_s.at[7 + d],
                    st_r.at[7 + d],
                    at_ctx(ctx + 64 - d),
                )
            )
        return copies

    st_list = st_copies()
    for copy in st_list:
        copy.start()
    for copy in st_list:
        copy.wait_recv()

    def gradient(j, _):
        stats = [rst[8 - j + t, j] for t in range(9)]
        peak = stats[0][0:1]
        for stat in stats[1:]:
            peak = jnp.maximum(peak, stat[0:1])
        total = jnp.zeros((8, 128), F32)
        for stat in stats:
            total = total + jnp.exp(stat[0:1] - peak) * stat
        filled = total[1:2] > 0.0
        scale = jnp.where(filled, 1.0 / jnp.where(filled, total[1:2], 1.0), 0.0)
        m = total[2:3] * scale
        a = total[3:4] * scale
        m_tan = total[4:5] * scale - a * m
        p = ev[j] * (jnp.exp(rst[8, j][0:1] - peak) * scale)
        rest = gv[j] - m
        ds = p * rest
        ds_tan = p * ((sv[j] - a) * rest - m_tan)
        high, low = split(jnp.concatenate([ds, ds_tan], axis=0))
        prod = dot_nn(jnp.concatenate([high, low], axis=0), qu[j, 0])
        acc[...] += prod[0:256] + prod[256:512]
        return 0

    acc[...] = jnp.zeros((256, 128), F32)
    lax.fori_loop(0, 9, gradient, 0)

    w = rope_back(acc[0:128] * SCORE_SCALE) * key_gain
    w_tan = rope_back(acc[128:256] * SCORE_SCALE) * key_gain
    xw = mean(lin * w)
    xw_tan = mean(tan * w) + mean(lin * w_tan)
    cot = (
        inv_tan * w
        + inv * w_tan
        - tan * (inv3 * xw)
        - lin * (3.0 * inv * inv * inv_tan * xw + inv3 * xw_tan)
    )
    cott[k] = jnp.transpose(cot).astype(BF16)
    cot_swap = rdma(cott.at[k], cott.at[k], one_s.at[2], one_r.at[2], other)
    cot_swap.start()
    cot_in = rdma(cott.at[1 - k], cott.at[1 - k], one_s.at[2], one_r.at[2], other)
    cot_in.wait_recv()
    cots = jnp.concatenate([cott[0], cott[1]], axis=1)

    def rx_copy(dx, yi):
        cols = pl.ds(pl.multiple_of(yi * 16, 16), 16)
        return rdma(
            tb.at[dx, cols], rx.at[dx - 1, cols], rx_s.at[dx - 1, yi], rx_r.at[dx - 1, yi], at_x((x + dx) % 4)
        )

    for dx in (2, 1, 3):
        tb[dx] = dot_nn(cots, nb[(x + dx) % 4]).astype(BF16)

    def rx_send(t, _):
        yi = (y + 4 + t) % 8
        for dx in (2, 1, 3):
            rx_copy(dx, yi).start()
        return 0

    lax.fori_loop(0, 8, rx_send, 0)
    kl_own = dot_nn(cots, nb[x])
    tb_own = kl_own.astype(F32)
    py[...] = tb_own

    def rx_sum(yi):
        cols = pl.ds(pl.multiple_of(yi * 16, 16), 16)
        total = py[cols, :]
        for dx in (2, 1, 3):
            rx_copy(dx, yi).wait_recv()
            total = total + rx[dx - 1, cols, :].astype(F32)
        return total

    def ry_copy(t, dy):
        yi = (y + dy) % 8
        cols = pl.ds(pl.multiple_of(yi * 16, 16), 16)
        return rdma(tb.at[0, cols], ry.at[dy], ry_s.at[dy - 1], ry_r.at[dy - 1], at_y(yi))

    def y_sum(t, _):
        dy = (4 + t) % 8
        yi = (y + dy) % 8
        total = rx_sum(yi)
        cols = pl.ds(pl.multiple_of(yi * 16, 16), 16)
        tb[0, cols, :] = total.astype(BF16)
        ry_copy(t, dy).start()
        return 0

    lax.fori_loop(0, 4, y_sum, 0)
    lax.fori_loop(5, 8, y_sum, 0)
    total = rx_sum(y)

    def y_add(dy, _):
        ry_copy(0, dy).wait_recv()
        return 0

    lax.fori_loop(1, 8, y_add, 0)
    for dy in range(1, 8):
        total = total + ry[dy].astype(F32)

    def pz_copy(slot, src_z):
        zi = k * 4 + slot // 2
        return rdma(pz.at[slot], rz.at[src_z], rz_s.at[slot], rz_r.at[src_z], at_z(zi, slot % 2))

    for slot in range(8):
        goal, lead = (ROWS * slot) // 128, (ROWS * slot) % 128
        piece = total[:, goal * 128 : goal * 128 + 128]
        if lead:
            piece = pltpu.roll(piece, 128 - lead, 1)
        if lead + ROWS > 128:
            following = pltpu.roll(total[:, goal * 128 + 128 : goal * 128 + 256], 128 - lead, 1)
            piece = jnp.where(lane128 < 128 - lead, piece, following)
        pz[slot] = jnp.where(lane128 < ROWS, piece, 0.0)

    def pz_self(slot):
        return jnp.logical_and(k * 4 + slot // 2 == z, slot % 2 == k)

    def pz_send(t, _):
        slot = (own_slot + 1 + t) % 8

        @pl.when(jnp.logical_not(pz_self(slot)))
        def _():
            pz_copy(slot, z).start()

        @pl.when(pz_self(slot))
        def _():
            rz[z] = pz[slot]

        return 0

    lax.fori_loop(0, 8, pz_send, 0)

    def rz_wait(t, _):
        src = (z + t) % 8

        @pl.when(jnp.logical_or(src != z, half != k))
        def _():
            pz_copy(0, src).wait_recv()

        return 0

    lax.fori_loop(0, 8, rz_wait, 0)
    product = rz[0]
    for src in range(1, 8):
        product = product + rz[src]
    product = product * D ** (-0.5)

    rows = [jnp.sum(bas[a] * product, axis=0, keepdims=True) for a in range(7)]
    rows.append(jnp.sum(product * product, axis=0, keepdims=True))
    sums = jnp.concatenate(rows + [gram], axis=0)

    def all_sum(stage, value, own, device):
        ar[stage, own] = value

        def copy(src, t, target):
            return rdma(
                ar.at[stage, src], ar.at[stage, src], ar_s.at[stage, t], ar_r.at[stage, src], device(target)
            )

        def send(t, _):
            copy(own, t, (own + far_step(t)) % 8).start()
            return 0

        lax.fori_loop(0, 7, send, 0)

        def wait(t, _):
            copy((own + ring_step(t)) % 8, 0, own).wait_recv()
            return 0

        lax.fori_loop(0, 7, wait, 0)
        total = ar[stage, 0]
        for i in range(1, 8):
            total = total + ar[stage, i]

        def drain(t, _):
            copy(own, t, (own + far_step(t)) % 8).wait_send()
            return 0

        lax.fori_loop(0, 7, drain, 0)
        return total

    sums = all_sum(0, sums, x * 2 + k, lambda i: (z * 8 + i, y))
    sums = all_sum(1, sums, z, lambda i: (i * 8 + x * 2 + k, y))
    sums = all_sum(2, sums, y, lambda i: (ctx, i))
    inner = jnp.sum(sums[0:8], axis=1, keepdims=True)
    coef = jnp.broadcast_to(inner / ENTRIES, (8, 128))
    coef_row = jnp.sum(jnp.where(jnp.logical_and(sub8 == lane8, sub8 < 7), coef, 0.0), axis=0, keepdims=True)
    quad = jnp.sum(coef_row * sums[8:16], axis=1, keepdims=True)
    norm = jnp.where(sub8 < 7, coef * (quad - 2.0 * inner), jnp.broadcast_to(inner, (8, 128)))
    squared = jnp.maximum(jnp.sum(norm, axis=0, keepdims=True), 0.0) / ENTRIES
    beta = jnp.sqrt(squared + EPSILON)
    residual = product
    for a in range(7):
        residual = residual - coef[a : a + 1] * bas[a]
    out[...] = residual / beta
    aux[...] = jnp.where(sub8 < 7, coef, jnp.broadcast_to(beta, (8, 128)))

    def g1_drain(t, _):
        zi = (z + t) % 8

        @pl.when(jnp.logical_or(zi != z, half != k))
        def _():
            g1_copy(zi, own_slot).wait_send()

        return 0

    lax.fori_loop(0, 8, g1_drain, 0)

    def qu_drain(j, _):
        qu_copy(j).wait_send()
        sg_copy(j).wait_send()
        return 0

    lax.fori_loop(1, 9, qu_drain, 0)

    def y_drain(t, _):
        y_copy(y, (y + far_step(t)) % 8, t).wait_send()
        ry_copy(0, t + 1).wait_send()
        return 0

    lax.fori_loop(0, 7, y_drain, 0)

    def x_drain(yi, _):
        for t, dx in enumerate((2, 1, 3)):
            x_copy(x, yi, (x + dx) % 4, t).wait_send()
            rx_copy(dx, yi).wait_send()
        return 0

    lax.fori_loop(0, 8, x_drain, 0)
    swap.wait_send()
    kl_swap.wait_send()
    cot_swap.wait_send()
    for copy in st_list:
        copy.wait_send()

    def pz_drain(slot, _):
        @pl.when(jnp.logical_not(pz_self(slot)))
        def _():
            pz_copy(slot, z).wait_send()

        return 0

    lax.fori_loop(0, 8, pz_drain, 0)


def body(
    tokens,
    norm_gain,
    queries,
    values,
    upstream,
    segments,
    key_weight,
    key_gain,
    direction,
    stored_basis,
):
    tangent = (direction * D ** (-0.5)).astype(BF16)
    pad = ((0, 0), (0, 0), (0, 128 - ROWS))
    wt = jnp.pad(jnp.stack([key_weight.T, tangent.T]), pad)
    stacked = jnp.concatenate([stored_basis, direction[None]], axis=0)
    bas = jnp.pad(jnp.swapaxes(stacked, 1, 2), pad)
    dma = pltpu.SemaphoreType.DMA
    vmem = pl.BlockSpec(memory_space=pltpu.VMEM)
    out, aux = pl.pallas_call(
        kernel,
        out_shape=(jax.ShapeDtypeStruct((16, 128), F32), jax.ShapeDtypeStruct((8, 128), F32)),
        in_specs=[vmem] * 10,
        out_specs=(vmem, vmem),
        scratch_shapes=[
            pltpu.VMEM((8, 2, 16, 128), BF16),
            pltpu.VMEM((4, 2, 128, GROUP), BF16),
            pltpu.VMEM((4, 256, GROUP), BF16),
            pltpu.VMEM((4, 128, GROUP), BF16),
            pltpu.VMEM((9, 2, 128, 128), BF16),
            pltpu.VMEM((9, 8, 128), jnp.int32),
            pltpu.VMEM((256, 256), F32),
            pltpu.VMEM((128, 256), F32),
            pltpu.VMEM((9, 128, 128), F32),
            pltpu.VMEM((9, 128, 128), F32),
            pltpu.VMEM((9, 128, 128), F32),
            pltpu.VMEM((17, 9, 8, 128), F32),
            pltpu.VMEM((2, 128, 128), BF16),
            pltpu.VMEM((256, 128), F32),
            pltpu.VMEM((4, 128, GROUP), BF16),
            pltpu.VMEM((3, 128, GROUP), BF16),
            pltpu.VMEM((128, GROUP), F32),
            pltpu.VMEM((8, 16, GROUP), BF16),
            pltpu.VMEM((8, 16, 128), F32),
            pltpu.VMEM((8, 16, 128), F32),
            pltpu.VMEM((3, 8, 16, 128), F32),
            pltpu.VMEM((2, 128, 128), F32),
            dma((8,)),
            dma((8,)),
            dma((8,)),
            dma((8,)),
            dma((8,)),
            dma((8,)),
            dma((7,)),
            dma((8,)),
            dma((3, 8)),
            dma((4, 8)),
            dma((3,)),
            dma((3,)),
            dma((16,)),
            dma((16,)),
            dma((3, 8)),
            dma((3, 8)),
            dma((7,)),
            dma((7,)),
            dma((8,)),
            dma((8,)),
            dma((3, 7)),
            dma((3, 8)),
        ],
        compiler_params=pltpu.CompilerParams(
            collective_id=0, has_side_effects=True, vmem_limit_bytes=56 * 2**20
        ),
        name="lanczos_step",
    )(
        tokens[0],
        norm_gain[None],
        queries[0],
        values[0],
        upstream[0],
        segments,
        wt,
        key_gain[None],
        jnp.asarray(FREQS),
        bas,
    )
    return aux[:7, 0], aux[7, 0], out[:, :ROWS].T


def solution(mesh):
    in_specs = (
        P("dp", "ctx", None),
        P(),
        P("dp", "ctx", None),
        P("dp", "ctx", None),
        P("dp", "ctx", None),
        P("dp", "ctx"),
        P("ctx", "dp"),
        P(),
        P("ctx", "dp"),
        P(None, "ctx", "dp"),
    )
    out_specs = (P(), P(), P("ctx", "dp"))
    return jax.shard_map(body, mesh=mesh, in_specs=in_specs, out_specs=out_specs, check_vma=False)
```

```python
import jax
import jax.numpy as jnp
import numpy as np
from jax import lax
from jax.experimental import pallas as pl
from jax.experimental.pallas import tpu as pltpu
from jax.sharding import PartitionSpec as P

D = 5376
HD = 128
WINDOW = 1024
HALF = D // 2
ROWS = 84
SCORE_SCALE = 168.0 ** (-0.5)
EPSILON = 1e-06
ENTRIES = D * HD
GROUP = 768
LOW = -1e30
MESH = pl.DeviceIdType.MESH
F32 = jnp.float32
BF16 = jnp.bfloat16
FREQS = np.tile(10000.0 ** (-np.arange(64) / 64.0), 2)[None].astype(np.float32)


def dot_nt(a, b):
    return lax.dot_general(a, b, (((1,), (1,)), ((), ())), preferred_element_type=F32)


def dot_nn(a, b):
    return lax.dot_general(a, b, (((1,), (0,)), ((), ())), preferred_element_type=F32)


def split(a):
    high = a.astype(BF16)
    return high, (a - high.astype(F32)).astype(BF16)


def ring_step(t):
    odd = t % 2
    return odd * (8 - (t + 1) // 2) + (1 - odd) * ((t + 2) // 2)


def far_step(t):
    return ring_step(6 - t)


def kernel(
    tok,
    gain,
    q_in,
    v_in,
    u_in,
    seg_in,
    w_in,
    dir_in,
    kg,
    freq_in,
    bas_in,
    out,
    coef_out,
    beta_out,
    wt,
    bas,
    g1,
    wb,
    nb,
    ns,
    qu,
    segb,
    kl,
    klr,
    ev,
    sv,
    gv,
    rst,
    cott,
    acc,
    tb,
    rx,
    py,
    ry,
    pz,
    rz,
    ar,
    cs,
    g1_s,
    g1_r,
    qu_s,
    qu_r,
    sg_s,
    sg_r,
    y_s,
    y_r,
    x_s,
    x_r,
    f_s,
    f_r,
    one_s,
    one_r,
    st_s,
    st_r,
    rx_s,
    rx_r,
    ry_s,
    ry_r,
    rz_s,
    rz_r,
    ar_s,
    ar_r,
):
    ctx = lax.axis_index("ctx")
    y = lax.axis_index("dp")
    z = ctx // 8
    x = (ctx // 2) % 4
    k = ctx % 2
    half = z // 4
    zz = z % 4
    parity = z % 2
    place = ctx % 8

    def at_z(zi, ki):
        return ((zi * 4 + x) * 2 + ki, y)

    def at_x(xi):
        return ((z * 4 + xi) * 2 + k, y)

    def at_y(yi):
        return (ctx, yi)

    def at_ctx(ci):
        return (ci % 64, y)

    other = ((z * 4 + x) * 2 + (1 - k), y)
    drains = []

    def rdma(src, dst, send, recv, device):
        return pltpu.make_async_remote_copy(
            src_ref=src,
            dst_ref=dst,
            send_sem=send,
            recv_sem=recv,
            device_id=device,
            device_id_type=MESH,
        )

    barrier = pltpu.get_barrier_semaphore()

    def greet(device):
        pl.semaphore_signal(barrier, inc=1, device_id=device, device_id_type=MESH)

    for d in range(1, 9):
        greet(at_ctx(ctx + d))
        greet(at_ctx(ctx + 64 - d))
    for dz in range(2, 7):
        greet(at_z((z + dz) % 8, 0))
        greet(at_z((z + dz) % 8, 1))
    for dz in (1, 7):
        greet(at_z((z + dz) % 8, 1 - k))
    for dy in range(1, 8):
        greet(at_y((y + dy) % 8))

    qu[0, 0] = q_in[...]
    qu[0, 1] = u_in[...]
    segb[0] = jnp.broadcast_to(seg_in[...], (8, 128))
    wt[...] = jnp.zeros((2, 16, 128), BF16)
    wt[0, :, 0:ROWS] = w_in[...]
    wt[1, :, 0:ROWS] = (dir_in[...] * D ** (-0.5)).astype(BF16)
    pl.semaphore_wait(barrier, 35)

    own_slot = zz * 2 + k

    def g1_copy(zi, slot):
        return rdma(wt.at[zi % 2], g1.at[slot], g1_s.at[zi], g1_r.at[slot], at_z(zi, half))

    def g1_send(t, _):
        zi = (z + t) % 8

        @pl.when(jnp.logical_or(zi != z, half != k))
        def _():
            g1_copy(zi, own_slot).start()

        return 0

    lax.fori_loop(0, 8, g1_send, 0)

    def g1_drain(t, _):
        zi = (z + t) % 8

        @pl.when(jnp.logical_or(zi != z, half != k))
        def _():
            g1_copy(zi, own_slot).wait_send()

        return 0

    drains.append(lambda: lax.fori_loop(0, 8, g1_drain, 0))

    @pl.when(half == k)
    def _():
        g1[own_slot] = wt[parity]

    bas[...] = jnp.zeros((7, 16, 128), F32)
    bas[0:6, :, 0:ROWS] = bas_in[...]
    bas[6, :, 0:ROWS] = dir_in[...]

    def qu_far():
        return [
            rdma(ref.at[0], ref.at[8], sends.at[7], recvs.at[7], at_ctx(ctx + 56))
            for ref, sends, recvs in ((qu, qu_s, qu_r), (segb, sg_s, sg_r))
        ]

    def qu_near(j):
        source = 8 * ((j + 7 - place) // 8)
        device = at_ctx(ctx + source + 64 - j)
        return [
            rdma(ref.at[source], ref.at[j], sends.at[j - 1], recvs.at[j - 1], device)
            for ref, sends, recvs in ((qu, qu_s, qu_r), (segb, sg_s, sg_r))
        ]

    for copy in qu_far():
        copy.start()
        drains.append(copy.wait_send)

    lane128 = lax.broadcasted_iota(jnp.int32, (1, 128), 1)
    gain_tiles = gain[...].astype(F32)
    gain_row = jnp.concatenate([gain_tiles[i : i + 1] for i in range(D // 128)], axis=1)

    def norm_chunk(r):
        rows = pl.ds(pl.multiple_of(r * 16, 16), 16)
        floats = tok[rows, :].astype(F32)
        scale = lax.rsqrt(jnp.mean(floats * floats, axis=-1, keepdims=True) + EPSILON)
        normed = floats * scale * gain_row
        for hh in range(2):
            for xi in range(4):
                tiles = [jnp.zeros((16, 128), F32) for _ in range(6)]
                for zi in range(4):
                    start = hh * HALF + zi * 672 + xi * 168
                    first = min(start // 128, D // 128 - 3)
                    shift = start - first * 128
                    goal, lead = (168 * zi) // 128, (168 * zi) % 128
                    slab = normed[:, first * 128 : first * 128 + 384]
                    moved = pltpu.roll(slab, (lead - shift) % 384, 1) if lead != shift else slab
                    for m in range(3):
                        low, high = lead - 128 * m, lead + 168 - 128 * m
                        if high <= 0 or low >= 128:
                            continue
                        part = moved[:, 128 * m : 128 * m + 128]
                        if low > 0 or high < 128:
                            inside = jnp.logical_and(lane128 >= low, lane128 < high)
                            part = jnp.where(inside, part, 0.0)
                        tiles[goal + m] = tiles[goal + m] + part
                group = jnp.concatenate(tiles, axis=1).astype(BF16)

                @pl.when(k == hh)
                def _():
                    nb[xi, pl.ds(pl.multiple_of(k * 128 + r * 16, 16), 16), :] = group

                @pl.when(k != hh)
                def _():
                    ns[xi, rows, :] = group

    norm_chunk(7)

    def g1_wait(slot, _):
        zi = half * 0 + k * 4 + slot // 2
        mine = jnp.logical_and(zi == z, slot % 2 == k)

        @pl.when(jnp.logical_not(mine))
        def _():
            g1_copy(z, slot).wait_recv()

        return 0

    lax.fori_loop(0, 8, g1_wait, 0)
    tiles = [jnp.zeros((16, 128), F32) for _ in range(6)]
    for slot in range(8):
        piece = g1[slot].astype(F32)
        goal, lead = (ROWS * slot) // 128, (ROWS * slot) % 128
        moved = pltpu.roll(piece, lead, 1) if lead else piece
        tiles[goal] = tiles[goal] + jnp.where(lane128 >= lead, moved, 0.0)
        if lead + ROWS > 128:
            tiles[goal + 1] = tiles[goal + 1] + jnp.where(lane128 < lead, moved, 0.0)
    wb[x, parity, pl.ds(pl.multiple_of(y * 16, 16), 16), :] = jnp.concatenate(tiles, axis=1).astype(BF16)

    def piece_at(matrix, xi, yi):
        return wb.at[xi, matrix, pl.ds(pl.multiple_of(yi * 16, 16), 16), :]

    def y_copy(src_y, dst_y, t):
        piece = piece_at(parity, x, src_y)
        return rdma(piece, piece, y_s.at[t], y_r.at[src_y], at_y(dst_y))

    def x_copy(src_x, yi, dst_x, t):
        piece = piece_at(parity, src_x, yi)
        return rdma(piece, piece, x_s.at[t, yi], x_r.at[src_x, yi], at_x(dst_x))

    def f_copy(matrix, xi, yi):
        piece = piece_at(matrix, xi, yi)
        target = at_z((z + 1 + 6 * (yi % 2)) % 8, k)
        return rdma(piece, piece, f_s.at[xi, yi], f_r.at[xi, yi], target)

    def y_send(t, _):
        y_copy(y, (y + far_step(t)) % 8, t).start()
        return 0

    lax.fori_loop(0, 7, y_send, 0)

    def y_drain(t, _):
        y_copy(y, (y + far_step(t)) % 8, t).wait_send()
        return 0

    drains.append(lambda: lax.fori_loop(0, 7, y_drain, 0))

    def x_send(yi):
        for t, dx in enumerate((2, 1, 3)):
            x_copy(x, yi, (x + dx) % 4, t).start()
        f_copy(parity, x, yi).start()

    x_send(y)
    for copy in qu_far():
        copy.wait_recv()

    def qu_send(j, _):
        for copy in qu_near(j):
            copy.start()
        return 0

    lax.fori_loop(1, 8, qu_send, 0)

    def qu_drain(j, _):
        for copy in qu_near(j):
            copy.wait_send()
        return 0

    drains.append(lambda: lax.fori_loop(1, 8, qu_drain, 0))

    def y_forward(t, _):
        norm_chunk(t)
        src = (y + ring_step(t)) % 8
        y_copy(src, y, 0).wait_recv()
        x_send(src)
        return 0

    lax.fori_loop(0, 7, y_forward, 0)

    def x_drain(yi, _):
        for t, dx in enumerate((2, 1, 3)):
            x_copy(x, yi, (x + dx) % 4, t).wait_send()
        for xi in range(4):
            f_copy(parity, xi, yi).wait_send()
        return 0

    drains.append(lambda: lax.fori_loop(0, 8, x_drain, 0))

    swap = rdma(
        ns, nb.at[:, pl.ds(pl.multiple_of(k * 128, 128), 128), :], one_s.at[0], one_r.at[0], other
    )
    swap.start()
    drains.append(swap.wait_send)

    def x_forward(t, _):
        yi = (y + ring_step(t - 1)) % 8
        for dx in (1, 3, 2):
            xi = (x + dx) % 4
            x_copy(xi, yi, x, 0).wait_recv()
            f_copy(parity, xi, yi).start()
        return 0

    lax.fori_loop(0, 8, x_forward, 0)

    lane = lax.broadcasted_iota(jnp.int32, (128, 128), 1)
    sub = lax.broadcasted_iota(jnp.int32, (128, 128), 0)
    angle = (ctx * 128 + sub).astype(F32) * freq_in[...]
    cs[0] = jnp.cos(angle)
    cs[1] = jnp.sin(angle) * jnp.where(lane < 64, -1.0, 1.0)
    key_doc = jnp.transpose(jnp.broadcast_to(segb[0, 0:1].astype(F32), (128, 128)))

    lane8 = lax.broadcasted_iota(jnp.int32, (8, 128), 1)
    sub8 = lax.broadcasted_iota(jnp.int32, (8, 128), 0)
    gram = jnp.zeros((8, 128), F32)
    for a in range(7):
        for b in range(a, 7):
            dotted = jnp.sum(jnp.sum(bas[a] * bas[b], axis=0, keepdims=True), axis=1, keepdims=True)
            spot = jnp.logical_and(sub8 == a, lane8 == b)
            if a != b:
                spot = jnp.logical_or(spot, jnp.logical_and(sub8 == b, lane8 == a))
            gram = jnp.where(spot, dotted, gram)

    swap.wait_recv()
    first = jnp.zeros((256, 128), F32)
    for xi in range(4):
        first = first + dot_nt(nb[xi], wb[xi, parity])
    kl[parity] = first
    second = jnp.zeros((256, 128), F32)
    for xi in range(4):

        def f_wait(yi, _):
            f_copy(1 - parity, xi, yi).wait_recv()
            return 0

        lax.fori_loop(0, 8, f_wait, 0)
        second = second + dot_nt(nb[xi], wb[xi, 1 - parity])
    kl[1 - parity] = second
    mine = pl.ds(pl.multiple_of(k * 128, 128), 128)
    theirs = pl.ds(pl.multiple_of((1 - k) * 128, 128), 128)
    kl_swap = rdma(kl.at[:, theirs], klr, one_s.at[1], one_r.at[1], other)
    kl_swap.start()
    drains.append(kl_swap.wait_send)

    def qu_wait(j, _):
        for copy in qu_near(j):
            copy.wait_recv()
        return 0

    lax.fori_loop(1, 8, qu_wait, 0)
    kl_swap.wait_recv()
    lin, tan = kl[0, mine] + klr[0], kl[1, mine] + klr[1]
    cosine, sine = cs[0], cs[1]
    key_gain = kg[...]

    def rope(vec):
        return vec * cosine + pltpu.roll(vec, 64, 1) * sine

    def rope_back(vec):
        return vec * cosine - pltpu.roll(vec, 64, 1) * sine

    def mean(vec):
        return jnp.mean(vec, axis=-1, keepdims=True)

    inv = lax.rsqrt(mean(lin * lin) + EPSILON)
    inv3 = inv * inv * inv
    inv_tan = -inv3 * mean(lin * tan)
    keyed = rope(lin * inv * key_gain) * SCORE_SCALE
    keyed_tan = rope((tan * inv + lin * inv_tan) * key_gain) * SCORE_SCALE
    k_high, k_low = split(keyed)
    t_high, t_low = split(keyed_tan)
    stacked_keys = jnp.concatenate([k_high, k_low, t_high, t_low], axis=0)
    value_rows = v_in[...]

    def score(j, _):
        raw = dot_nt(stacked_keys, qu[j, 0])
        s = raw[0:128] + raw[128:256]
        st = raw[256:384] + raw[384:512]
        g = dot_nt(value_rows, qu[j, 1])
        gap = 128 * j + lane - sub
        near = jnp.logical_and(gap >= 0, gap < WINDOW)
        same = key_doc == segb[j, 0:1].astype(F32)
        allowed = jnp.logical_and(jnp.logical_and(near, same), ctx + j < 64)
        top = jnp.max(jnp.where(allowed, s, LOW), axis=0, keepdims=True)
        e = jnp.where(allowed, jnp.exp(s - top), 0.0)
        est = e * st
        rows = [top] + [jnp.sum(m, axis=0, keepdims=True) for m in (e, e * g, est, est * g)]
        rst[8, j] = jnp.concatenate(rows + [jnp.zeros((3, 128), F32)], axis=0)
        ev[j] = e
        sv[j] = st
        gv[j] = g
        return 0

    lax.fori_loop(0, 9, score, 0)

    def st_copies():
        copies = []
        for d in range(1, 9):
            n = 9 - d
            copies.append(
                rdma(
                    rst.at[8, pl.ds(d, n)],
                    rst.at[8 + d, pl.ds(0, n)],
                    st_s.at[d - 1],
                    st_r.at[d - 1],
                    at_ctx(ctx + d),
                )
            )
            copies.append(
                rdma(
                    rst.at[8, pl.ds(0, n)],
                    rst.at[8 - d, pl.ds(d, n)],
                    st_s.at[7 + d],
                    st_r.at[7 + d],
                    at_ctx(ctx + 64 - d),
                )
            )
        return copies

    st_list = st_copies()
    for copy in st_list:
        copy.start()
        drains.append(copy.wait_send)
    for copy in st_list:
        copy.wait_recv()

    def gradient(j, _):
        stats = [rst[8 - j + t, j] for t in range(9)]
        peak = stats[0][0:1]
        for stat in stats[1:]:
            peak = jnp.maximum(peak, stat[0:1])
        total = jnp.zeros((8, 128), F32)
        for stat in stats:
            total = total + jnp.exp(stat[0:1] - peak) * stat
        filled = total[1:2] > 0.0
        scale = jnp.where(filled, 1.0 / jnp.where(filled, total[1:2], 1.0), 0.0)
        m = total[2:3] * scale
        a = total[3:4] * scale
        m_tan = total[4:5] * scale - a * m
        p = ev[j] * (jnp.exp(rst[8, j][0:1] - peak) * scale)
        rest = gv[j] - m
        ds = p * rest
        ds_tan = p * ((sv[j] - a) * rest - m_tan)
        high, low = split(jnp.concatenate([ds, ds_tan], axis=0))
        prod = dot_nn(jnp.concatenate([high, low], axis=0), qu[j, 0])
        acc[...] += prod[0:256] + prod[256:512]
        return 0

    acc[...] = jnp.zeros((256, 128), F32)
    lax.fori_loop(0, 9, gradient, 0)

    w = rope_back(acc[0:128] * SCORE_SCALE) * key_gain
    w_tan = rope_back(acc[128:256] * SCORE_SCALE) * key_gain
    xw = mean(lin * w)
    xw_tan = mean(tan * w) + mean(lin * w_tan)
    cot = (
        inv_tan * w
        + inv * w_tan
        - tan * (inv3 * xw)
        - lin * (3.0 * inv * inv * inv_tan * xw + inv3 * xw_tan)
    )
    cott[k] = jnp.transpose(cot).astype(BF16)
    cot_swap = rdma(cott.at[k], cott.at[k], one_s.at[2], one_r.at[2], other)
    cot_swap.start()
    drains.append(cot_swap.wait_send)
    cot_in = rdma(cott.at[1 - k], cott.at[1 - k], one_s.at[2], one_r.at[2], other)
    cot_in.wait_recv()
    cots = jnp.concatenate([cott[0], cott[1]], axis=1)

    def rx_copy(dx, yi):
        cols = pl.ds(pl.multiple_of(yi * 16, 16), 16)
        return rdma(
            tb.at[dx, cols], rx.at[dx - 1, cols], rx_s.at[dx - 1, yi], rx_r.at[dx - 1, yi], at_x((x + dx) % 4)
        )

    for dx in (2, 1, 3):
        tb[dx] = dot_nn(cots, nb[(x + dx) % 4]).astype(BF16)

    def rx_send(t, _):
        yi = (y + far_step(t)) % 8
        for dx in (2, 1, 3):
            rx_copy(dx, yi).start()
        return 0

    lax.fori_loop(0, 8, rx_send, 0)

    def rx_drain(yi, _):
        for dx in (2, 1, 3):
            rx_copy(dx, yi).wait_send()
        return 0

    drains.append(lambda: lax.fori_loop(0, 8, rx_drain, 0))
    py[...] = dot_nn(cots, nb[x])

    def rx_sum(yi):
        cols = pl.ds(pl.multiple_of(yi * 16, 16), 16)
        total = py[cols, :]
        for dx in (2, 1, 3):
            rx_copy(dx, yi).wait_recv()
            total = total + rx[dx - 1, cols, :].astype(F32)
        return total

    def ry_copy(t, dy):
        yi = (y + dy) % 8
        cols = pl.ds(pl.multiple_of(yi * 16, 16), 16)
        return rdma(tb.at[0, cols], ry.at[dy], ry_s.at[dy - 1], ry_r.at[dy - 1], at_y(yi))

    def y_sum(t, _):
        dy = far_step(t)
        yi = (y + dy) % 8
        total = rx_sum(yi)
        cols = pl.ds(pl.multiple_of(yi * 16, 16), 16)
        tb[0, cols, :] = total.astype(BF16)
        ry_copy(t, dy).start()
        return 0

    lax.fori_loop(0, 7, y_sum, 0)

    def ry_drain(t, _):
        ry_copy(0, t + 1).wait_send()
        return 0

    drains.append(lambda: lax.fori_loop(0, 7, ry_drain, 0))
    total = rx_sum(y)

    def y_add(dy, _):
        ry_copy(0, dy).wait_recv()
        return 0

    lax.fori_loop(1, 8, y_add, 0)
    for dy in range(1, 8):
        total = total + ry[dy].astype(F32)

    def pz_copy(slot, src_z):
        zi = k * 4 + slot // 2
        return rdma(pz.at[slot], rz.at[src_z], rz_s.at[slot], rz_r.at[src_z], at_z(zi, slot % 2))

    for slot in range(8):
        goal, lead = (ROWS * slot) // 128, (ROWS * slot) % 128
        piece = total[:, goal * 128 : goal * 128 + 128]
        if lead:
            piece = pltpu.roll(piece, 128 - lead, 1)
        if lead + ROWS > 128:
            following = pltpu.roll(total[:, goal * 128 + 128 : goal * 128 + 256], 128 - lead, 1)
            piece = jnp.where(lane128 < 128 - lead, piece, following)
        pz[slot] = jnp.where(lane128 < ROWS, piece, 0.0)

    def pz_self(slot):
        return jnp.logical_and(k * 4 + slot // 2 == z, slot % 2 == k)

    def pz_send(t, _):
        slot = (own_slot + 1 + t) % 8

        @pl.when(jnp.logical_not(pz_self(slot)))
        def _():
            pz_copy(slot, z).start()

        @pl.when(pz_self(slot))
        def _():
            rz[z] = pz[slot]

        return 0

    lax.fori_loop(0, 8, pz_send, 0)

    def pz_drain(slot, _):
        @pl.when(jnp.logical_not(pz_self(slot)))
        def _():
            pz_copy(slot, z).wait_send()

        return 0

    drains.append(lambda: lax.fori_loop(0, 8, pz_drain, 0))

    def rz_wait(t, _):
        src = (z + t) % 8

        @pl.when(jnp.logical_or(src != z, half != k))
        def _():
            pz_copy(0, src).wait_recv()

        return 0

    lax.fori_loop(0, 8, rz_wait, 0)
    product = rz[0]
    for src in range(1, 8):
        product = product + rz[src]
    product = product * D ** (-0.5)

    rows = [jnp.sum(bas[a] * product, axis=0, keepdims=True) for a in range(7)]
    rows.append(jnp.sum(product * product, axis=0, keepdims=True))
    sums = jnp.concatenate(rows + [gram], axis=0)

    def all_sum(stage, value, own, device):
        ar[stage, own] = value

        def copy(src, t, target):
            return rdma(
                ar.at[stage, src], ar.at[stage, src], ar_s.at[stage, t], ar_r.at[stage, src], device(target)
            )

        def send(t, _):
            copy(own, t, (own + far_step(t)) % 8).start()
            return 0

        lax.fori_loop(0, 7, send, 0)

        def wait(t, _):
            copy((own + ring_step(t)) % 8, 0, own).wait_recv()
            return 0

        lax.fori_loop(0, 7, wait, 0)
        total = ar[stage, 0]
        for i in range(1, 8):
            total = total + ar[stage, i]

        def drain(t, _):
            copy(own, t, (own + far_step(t)) % 8).wait_send()
            return 0

        drains.append(lambda: lax.fori_loop(0, 7, drain, 0))
        return total

    sums = all_sum(0, sums, x * 2 + k, lambda i: (z * 8 + i, y))
    sums = all_sum(1, sums, z, lambda i: (i * 8 + x * 2 + k, y))
    sums = all_sum(2, sums, y, lambda i: (ctx, i))
    inner = jnp.sum(sums[0:8], axis=1, keepdims=True)
    coef = jnp.broadcast_to(inner / ENTRIES, (8, 128))
    coef_row = jnp.sum(jnp.where(jnp.logical_and(sub8 == lane8, sub8 < 7), coef, 0.0), axis=0, keepdims=True)
    quad = jnp.sum(coef_row * sums[8:16], axis=1, keepdims=True)
    norm = jnp.where(sub8 < 7, coef * (quad - 2.0 * inner), jnp.broadcast_to(inner, (8, 128)))
    squared = jnp.maximum(jnp.sum(norm, axis=0, keepdims=True), 0.0) / ENTRIES
    beta = jnp.sqrt(squared + EPSILON)
    residual = product
    for a in range(7):
        residual = residual - coef[a : a + 1] * bas[a]
    out[...] = (residual / beta)[:, 0:ROWS]
    coef_out[...] = coef_row[:, 0:7]
    beta_out[...] = beta[:, 0:1]

    for drain in drains:
        drain()


def body(
    tokens,
    norm_gain,
    queries,
    values,
    upstream,
    segments,
    key_weight,
    key_gain,
    direction,
    stored_basis,
):
    dma = pltpu.SemaphoreType.DMA
    vmem = pl.BlockSpec(memory_space=pltpu.VMEM)
    out, coefficients, beta = pl.pallas_call(
        kernel,
        out_shape=tuple(jax.ShapeDtypeStruct(shape, F32) for shape in ((16, ROWS), (1, 7), (1, 1))),
        in_specs=[vmem] * 11,
        out_specs=(vmem,) * 3,
        scratch_shapes=[
            pltpu.VMEM((2, 16, 128), BF16),
            pltpu.VMEM((7, 16, 128), F32),
            pltpu.VMEM((8, 16, 128), BF16),
            pltpu.VMEM((4, 2, 128, GROUP), BF16),
            pltpu.VMEM((4, 256, GROUP), BF16),
            pltpu.VMEM((4, 128, GROUP), BF16),
            pltpu.VMEM((9, 2, 128, 128), BF16),
            pltpu.VMEM((9, 8, 128), jnp.int32),
            pltpu.VMEM((2, 256, 128), F32),
            pltpu.VMEM((2, 128, 128), F32),
            pltpu.VMEM((9, 128, 128), F32),
            pltpu.VMEM((9, 128, 128), F32),
            pltpu.VMEM((9, 128, 128), F32),
            pltpu.VMEM((17, 9, 8, 128), F32),
            pltpu.VMEM((2, 128, 128), BF16),
            pltpu.VMEM((256, 128), F32),
            pltpu.VMEM((4, 128, GROUP), BF16),
            pltpu.VMEM((3, 128, GROUP), BF16),
            pltpu.VMEM((128, GROUP), F32),
            pltpu.VMEM((8, 16, GROUP), BF16),
            pltpu.VMEM((8, 16, 128), F32),
            pltpu.VMEM((8, 16, 128), F32),
            pltpu.VMEM((3, 8, 16, 128), F32),
            pltpu.VMEM((2, 128, 128), F32),
            dma((8,)),
            dma((8,)),
            dma((8,)),
            dma((8,)),
            dma((8,)),
            dma((8,)),
            dma((7,)),
            dma((8,)),
            dma((3, 8)),
            dma((4, 8)),
            dma((4, 8)),
            dma((4, 8)),
            dma((3,)),
            dma((3,)),
            dma((16,)),
            dma((16,)),
            dma((3, 8)),
            dma((3, 8)),
            dma((7,)),
            dma((7,)),
            dma((8,)),
            dma((8,)),
            dma((3, 7)),
            dma((3, 8)),
        ],
        compiler_params=pltpu.CompilerParams(
            collective_id=0, has_side_effects=True, vmem_limit_bytes=56 * 2**20
        ),
        name="lanczos_step",
    )(
        tokens[0],
        norm_gain.reshape(D // 128, 128),
        queries[0],
        values[0],
        upstream[0],
        segments,
        key_weight.T,
        direction.T,
        key_gain[None],
        jnp.asarray(FREQS),
        jnp.swapaxes(stored_basis, 1, 2),
    )
    return coefficients.reshape(7), beta.reshape(()), out.T


def solution(mesh):
    in_specs = (
        P("dp", "ctx", None),
        P(),
        P("dp", "ctx", None),
        P("dp", "ctx", None),
        P("dp", "ctx", None),
        P("dp", "ctx"),
        P("ctx", "dp"),
        P(),
        P("ctx", "dp"),
        P(None, "ctx", "dp"),
    )
    out_specs = (P(), P(), P("ctx", "dp"))
    return jax.shard_map(body, mesh=mesh, in_specs=in_specs, out_specs=out_specs, check_vma=False)
```

```python
import jax
import jax.numpy as jnp
import numpy as np
from jax import lax
from jax.experimental import pallas as pl
from jax.experimental.pallas import tpu as pltpu
from jax.sharding import PartitionSpec as P

D = 5376
HD = 128
WINDOW = 1024
HALF = D // 2
ROWS = 84
SCORE_SCALE = 168.0 ** (-0.5)
EPSILON = 1e-06
ENTRIES = D * HD
GROUP = 768
CUT = 512
LOW = -1e30
MESH = pl.DeviceIdType.MESH
F32 = jnp.float32
BF16 = jnp.bfloat16
FREQS = np.tile(10000.0 ** (-np.arange(64) / 64.0), 2)[None].astype(np.float32)


def placement(xi):
    spans = {}
    for zi in range(4):
        start = (zi * 672 + xi * 168) % 128
        for m in range((start + 167) // 128 + 1):
            spans[zi, m] = (max(start - 128 * m, 0), min(start + 168 - 128 * m, 128))
    heads = sorted((span[1], key) for key, span in spans.items() if span[0] == 0 and span[1] < 128)
    tails = sorted((span[0], key) for key, span in spans.items() if span[0] > 0)
    tiles, free = {}, 0
    for end, key in reversed(heads):
        fits = [tail for tail in tails if tail[0] >= end]
        tiles[key] = free
        if fits:
            tails.remove(fits[0])
            tiles[fits[0][1]] = free
        free += 1
    for key in [tail[1] for tail in tails] + [key for key, span in spans.items() if span == (0, 128)]:
        tiles[key] = free
        free += 1
    return spans, tiles


def dot_nt(a, b):
    return lax.dot_general(a, b, (((1,), (1,)), ((), ())), preferred_element_type=F32)


def dot_nn(a, b):
    return lax.dot_general(a, b, (((1,), (0,)), ((), ())), preferred_element_type=F32)


def split(a):
    high = a.astype(BF16)
    return high, (a - high.astype(F32)).astype(BF16)


def ring_step(t):
    odd = t % 2
    return odd * (8 - (t + 1) // 2) + (1 - odd) * ((t + 2) // 2)


def far_step(t):
    return ring_step(6 - t)


def kernel(
    tok_in,
    gain,
    q_in,
    v_in,
    u_in,
    seg_in,
    w_in,
    dir_in,
    kg,
    freq_in,
    bas_in,
    out,
    coef_out,
    beta_out,
    tok,
    wt,
    bas,
    g1,
    wb,
    nb,
    ns,
    qu,
    segb,
    kl,
    klr,
    ev,
    sv,
    gv,
    rst,
    cott,
    acc,
    ta,
    tb,
    rx,
    py,
    ry,
    sy,
    sx,
    pz,
    rz,
    ar,
    cs,
    g1_s,
    g1_r,
    qu_s,
    qu_r,
    sg_s,
    sg_r,
    y_s,
    y_r,
    x_s,
    x_r,
    f_s,
    f_r,
    one_s,
    one_r,
    tok_s,
    st_s,
    st_r,
    rx_s,
    rx_r,
    ry_s,
    ry_r,
    sy_s,
    sy_r,
    sx_s,
    sx_r,
    rz_s,
    rz_r,
    ar_s,
    ar_r,
):
    ctx = lax.axis_index("ctx")
    y = lax.axis_index("dp")
    z = ctx // 8
    x = (ctx // 2) % 4
    k = ctx % 2
    half = z // 4
    zz = z % 4
    parity = z % 2

    def at_z(zi, ki):
        return ((zi * 4 + x) * 2 + ki, y)

    def at_x(xi):
        return ((z * 4 + xi) * 2 + k, y)

    def at_y(yi):
        return (ctx, yi)

    def at_ctx(ci):
        return (ci % 64, y)

    other = ((z * 4 + x) * 2 + (1 - k), y)
    drains = []

    def finish():
        while drains:
            drains.pop()()


    def rdma(src, dst, send, recv, device):
        return pltpu.make_async_remote_copy(
            src_ref=src,
            dst_ref=dst,
            send_sem=send,
            recv_sem=recv,
            device_id=device,
            device_id_type=MESH,
        )

    tok_copy = pltpu.make_async_copy(tok_in, tok, tok_s)
    tok_copy.start()

    barrier = pltpu.get_barrier_semaphore()

    def greet(device):
        pl.semaphore_signal(barrier, inc=1, device_id=device, device_id_type=MESH)

    for d in range(1, 9):
        greet(at_ctx(ctx + d))
        greet(at_ctx(ctx + 64 - d))
    for dz in range(2, 7):
        greet(at_z((z + dz) % 8, 0))
        greet(at_z((z + dz) % 8, 1))
    for dz in (1, 7):
        greet(at_z((z + dz) % 8, 1 - k))
    for dy in range(1, 8):
        greet(at_y((y + dy) % 8))

    qu[0, 0] = q_in[...]
    qu[0, 1] = u_in[...]
    segb[0] = jnp.broadcast_to(seg_in[...], (8, 128))
    wt[...] = jnp.zeros((2, 16, 128), BF16)
    wt[0, :, 0:ROWS] = w_in[...]
    wt[1, :, 0:ROWS] = (dir_in[...] * D ** (-0.5)).astype(BF16)
    pl.semaphore_wait(barrier, 35)

    own_slot = zz * 2 + k

    def g1_copy(zi, slot):
        return rdma(wt.at[zi % 2], g1.at[slot], g1_s.at[zi], g1_r.at[slot], at_z(zi, half))

    def g1_send(t, _):
        zi = (z + t) % 8

        @pl.when(jnp.logical_or(zi != z, half != k))
        def _():
            g1_copy(zi, own_slot).start()

        return 0

    lax.fori_loop(0, 8, g1_send, 0)

    def g1_drain(t, _):
        zi = (z + t) % 8

        @pl.when(jnp.logical_or(zi != z, half != k))
        def _():
            g1_copy(zi, own_slot).wait_send()

        return 0

    drains.append(lambda: lax.fori_loop(0, 8, g1_drain, 0))

    @pl.when(half == k)
    def _():
        g1[own_slot] = wt[parity]

    bas[...] = jnp.zeros((7, 16, 128), F32)
    bas[0:6, :, 0:ROWS] = bas_in[...]
    bas[6, :, 0:ROWS] = dir_in[...]

    def qu_far():
        return [
            rdma(ref.at[0], ref.at[8], sends.at[7], recvs.at[7], at_ctx(ctx + 56))
            for ref, sends, recvs in ((qu, qu_s, qu_r), (segb, sg_s, sg_r))
        ]

    def qu_pair(source, j, device):
        return [
            rdma(ref.at[source], ref.at[j], sends.at[j - 1], recvs.at[j - 1], device)
            for ref, sends, recvs in ((qu, qu_s, qu_r), (segb, sg_s, sg_r))
        ]

    def qu_chip(dx):
        return qu_pair(8 * (1 - (x + dx) // 4), 8 - 2 * dx, at_x((x + dx) % 4))

    def qu_core():
        return qu_pair(8 * (1 - k), 7 - 6 * k, other)

    def qu_next(dx):
        return qu_pair(8 - 2 * dx, 7 - 2 * dx + 2 * k, other)

    for copy in qu_far():
        copy.start()
        drains.append(copy.wait_send)

    lane128 = lax.broadcasted_iota(jnp.int32, (1, 128), 1)
    gain_tiles = gain[...].astype(F32)
    gain_row = jnp.concatenate([gain_tiles[i : i + 1] for i in range(D // 128)], axis=1)

    def norm_chunk(r):
        rows = pl.ds(pl.multiple_of(r * 16, 16), 16)
        floats = tok[rows, :].astype(F32)
        scale = lax.rsqrt(jnp.mean(floats * floats, axis=-1, keepdims=True) + EPSILON)
        normed = floats * scale * gain_row
        for hh in range(2):
            for xi in range(4):
                spans, tiles = placement(xi)
                columns = [None] * 6
                for key, (low, high) in spans.items():
                    source = (hh * HALF + key[0] * 672 + xi * 168) // 128 + key[1]
                    part = normed[:, source * 128 : source * 128 + 128]
                    held = columns[tiles[key]]
                    if held is not None:
                        part = jnp.where(lane128 < high, part, held) if low == 0 else jnp.where(lane128 >= low, part, held)
                    columns[tiles[key]] = part
                group = jnp.concatenate(columns, axis=1).astype(BF16)

                @pl.when(k == hh)
                def _():
                    nb[xi, pl.ds(pl.multiple_of(k * 128 + r * 16, 16), 16), :] = group

                @pl.when(k != hh)
                def _():
                    ns[xi, rows, :] = group

    tok_copy.wait()

    def norm(r, _):
        norm_chunk(r)
        return 0

    lax.fori_loop(0, 8, norm, 0)
    swap = rdma(
        ns, nb.at[:, pl.ds(pl.multiple_of(k * 128, 128), 128), :], one_s.at[0], one_r.at[0], other
    )
    swap.start()
    drains.append(swap.wait_send)


    def g1_wait(slot, _):
        zi = half * 0 + k * 4 + slot // 2
        mine = jnp.logical_and(zi == z, slot % 2 == k)

        @pl.when(jnp.logical_not(mine))
        def _():
            g1_copy(z, slot).wait_recv()

        return 0

    lax.fori_loop(0, 8, g1_wait, 0)
    for xi in range(4):

        @pl.when(x == xi)
        def _():
            tiles = placement(xi)[1]
            columns = [jnp.zeros((16, 128), F32) for _ in range(6)]
            for slot in range(8):
                piece = g1[slot].astype(F32)
                start = (slot // 2 * 672 + xi * 168) % 128 + slot % 2 * ROWS
                m, lead = start // 128, start % 128
                moved = pltpu.roll(piece, lead, 1) if lead else piece
                tile = tiles[slot // 2, m]
                columns[tile] = columns[tile] + jnp.where(lane128 >= lead, moved, 0.0)
                if lead + ROWS > 128:
                    tile = tiles[slot // 2, m + 1]
                    columns[tile] = columns[tile] + jnp.where(lane128 < lead, moved, 0.0)
            own = pl.ds(pl.multiple_of(y * 16, 16), 16)
            wb[xi, parity, own, :] = jnp.concatenate(columns, axis=1).astype(BF16)

    def piece_at(matrix, xi, yi):
        return wb.at[xi, matrix, pl.ds(pl.multiple_of(yi * 16, 16), 16), :]

    def y_copy(src_y, dst_y, t):
        piece = piece_at(parity, x, src_y)
        return rdma(piece, piece, y_s.at[t], y_r.at[src_y], at_y(dst_y))

    def x_copy(src_x, yi, dst_x, t):
        piece = piece_at(parity, src_x, yi)
        return rdma(piece, piece, x_s.at[t, yi], x_r.at[src_x, yi], at_x(dst_x))

    def f_copy(matrix, xi, yi):
        piece = piece_at(matrix, xi, yi)
        target = at_z((z + 1 + 6 * (yi % 2)) % 8, k)
        return rdma(piece, piece, f_s.at[xi, yi], f_r.at[xi, yi], target)

    def y_send(t, _):
        y_copy(y, (y + far_step(t)) % 8, t).start()
        return 0

    lax.fori_loop(0, 7, y_send, 0)

    def y_drain(t, _):
        y_copy(y, (y + far_step(t)) % 8, t).wait_send()
        return 0

    drains.append(lambda: lax.fori_loop(0, 7, y_drain, 0))

    def x_send(yi):
        for t, dx in enumerate((2, 1, 3)):
            x_copy(x, yi, (x + dx) % 4, t).start()
        f_copy(parity, x, yi).start()

    x_send(y)
    lane = lax.broadcasted_iota(jnp.int32, (128, 128), 1)
    sub = lax.broadcasted_iota(jnp.int32, (128, 128), 0)
    angle = (ctx * 128 + sub).astype(F32) * freq_in[...]
    cs[0] = jnp.cos(angle)
    cs[1] = jnp.sin(angle) * jnp.where(lane < 64, -1.0, 1.0)
    key_doc = jnp.transpose(jnp.broadcast_to(segb[0, 0:1].astype(F32), (128, 128)))

    def y_forward(t, _):
        src = (y + ring_step(t)) % 8
        y_copy(src, y, 0).wait_recv()
        x_send(src)
        return 0

    lax.fori_loop(0, 7, y_forward, 0)

    for copy in qu_far():
        copy.wait_recv()

    for dx in (2, 1, 3):
        for copy in qu_chip(dx):
            copy.start()
            drains.append(copy.wait_send)
    for copy in qu_core():
        copy.start()
        drains.append(copy.wait_send)

    def x_drain(yi, _):
        for t, dx in enumerate((2, 1, 3)):
            x_copy(x, yi, (x + dx) % 4, t).wait_send()
        for xi in range(4):
            f_copy(parity, xi, yi).wait_send()
        return 0

    drains.append(lambda: lax.fori_loop(0, 8, x_drain, 0))

    def x_forward(t, _):
        yi = (y + ring_step(t - 1)) % 8
        for dx in (1, 3, 2):
            xi = (x + dx) % 4
            x_copy(xi, yi, x, 0).wait_recv()
            f_copy(parity, xi, yi).start()
        return 0

    lax.fori_loop(0, 8, x_forward, 0)

    for dx in (1, 3, 2):
        for copy in qu_chip(dx):
            copy.wait_recv()
        for copy in qu_next(dx):
            copy.start()
            drains.append(copy.wait_send)

    swap.wait_recv()
    first = jnp.zeros((256, 128), F32)
    for xi in range(4):
        first = first + dot_nt(nb[xi], wb[xi, parity])
    kl[parity] = first
    second = jnp.zeros((256, 128), F32)
    for xi in range(4):

        def f_wait(yi, _):
            f_copy(1 - parity, xi, yi).wait_recv()
            return 0

        lax.fori_loop(0, 8, f_wait, 0)
        second = second + dot_nt(nb[xi], wb[xi, 1 - parity])
    kl[1 - parity] = second
    mine = pl.ds(pl.multiple_of(k * 128, 128), 128)
    theirs = pl.ds(pl.multiple_of((1 - k) * 128, 128), 128)
    kl_swap = rdma(kl.at[:, theirs], klr, one_s.at[1], one_r.at[1], other)
    kl_swap.start()
    drains.append(kl_swap.wait_send)

    for j in range(1, 8, 2):
        for copy in qu_pair(0, j, other):
            copy.wait_recv()
    kl_swap.wait_recv()
    lin, tan = kl[0, mine] + klr[0], kl[1, mine] + klr[1]
    cosine, sine = cs[0], cs[1]
    key_gain = kg[...]

    def rope(vec):
        return vec * cosine + pltpu.roll(vec, 64, 1) * sine

    def rope_back(vec):
        return vec * cosine - pltpu.roll(vec, 64, 1) * sine

    def mean(vec):
        return jnp.mean(vec, axis=-1, keepdims=True)

    inv = lax.rsqrt(mean(lin * lin) + EPSILON)
    inv3 = inv * inv * inv
    inv_tan = -inv3 * mean(lin * tan)
    keyed = rope(lin * inv * key_gain) * SCORE_SCALE
    keyed_tan = rope((tan * inv + lin * inv_tan) * key_gain) * SCORE_SCALE
    k_high, k_low = split(keyed)
    t_high, t_low = split(keyed_tan)
    stacked_keys = jnp.concatenate([k_high, k_low, t_high, t_low], axis=0)
    value_rows = v_in[...]

    def score(j, _):
        raw = dot_nt(stacked_keys, qu[j, 0])
        s = raw[0:128] + raw[128:256]
        st = raw[256:384] + raw[384:512]
        g = dot_nt(value_rows, qu[j, 1])
        gap = 128 * j + lane - sub
        near = jnp.logical_and(gap >= 0, gap < WINDOW)
        same = key_doc == segb[j, 0:1].astype(F32)
        allowed = jnp.logical_and(jnp.logical_and(near, same), ctx + j < 64)
        top = jnp.max(jnp.where(allowed, s, LOW), axis=0, keepdims=True)
        e = jnp.where(allowed, jnp.exp(s - top), 0.0)
        est = e * st
        rows = [top] + [jnp.sum(m, axis=0, keepdims=True) for m in (e, e * g, est, est * g)]
        rst[8, j] = jnp.concatenate(rows + [jnp.zeros((3, 128), F32)], axis=0)
        ev[j] = e
        sv[j] = st
        gv[j] = g
        return 0

    for j in range(9):
        score(j, 0)

    def st_copies():
        copies = []
        for d in range(1, 9):
            n = 9 - d
            copies.append(
                rdma(
                    rst.at[8, pl.ds(d, n)],
                    rst.at[8 + d, pl.ds(0, n)],
                    st_s.at[d - 1],
                    st_r.at[d - 1],
                    at_ctx(ctx + d),
                )
            )
            copies.append(
                rdma(
                    rst.at[8, pl.ds(0, n)],
                    rst.at[8 - d, pl.ds(d, n)],
                    st_s.at[7 + d],
                    st_r.at[7 + d],
                    at_ctx(ctx + 64 - d),
                )
            )
        return copies

    st_list = st_copies()
    for copy in st_list:
        copy.start()
        drains.append(copy.wait_send)
    lane8 = lax.broadcasted_iota(jnp.int32, (8, 128), 1)
    sub8 = lax.broadcasted_iota(jnp.int32, (8, 128), 0)
    gram = jnp.zeros((8, 128), F32)
    for a in range(7):
        for b in range(a, 7):
            dotted = jnp.sum(jnp.sum(bas[a] * bas[b], axis=0, keepdims=True), axis=1, keepdims=True)
            spot = jnp.logical_and(sub8 == a, lane8 == b)
            if a != b:
                spot = jnp.logical_or(spot, jnp.logical_and(sub8 == b, lane8 == a))
            gram = jnp.where(spot, dotted, gram)

    for copy in st_list:
        copy.wait_recv()

    def gradient(j, _):
        stats = [rst[8 - j + t, j] for t in range(9)]
        peak = stats[0][0:1]
        for stat in stats[1:]:
            peak = jnp.maximum(peak, stat[0:1])
        total = jnp.zeros((8, 128), F32)
        for stat in stats:
            total = total + jnp.exp(stat[0:1] - peak) * stat
        filled = total[1:2] > 0.0
        scale = jnp.where(filled, 1.0 / jnp.where(filled, total[1:2], 1.0), 0.0)
        m = total[2:3] * scale
        a = total[3:4] * scale
        m_tan = total[4:5] * scale - a * m
        p = ev[j] * (jnp.exp(rst[8, j][0:1] - peak) * scale)
        rest = gv[j] - m
        ds = p * rest
        ds_tan = p * ((sv[j] - a) * rest - m_tan)
        high, low = split(jnp.concatenate([ds, ds_tan], axis=0))
        prod = dot_nn(jnp.concatenate([high, low], axis=0), qu[j, 0])
        acc[...] += prod[0:256] + prod[256:512]
        return 0

    acc[...] = jnp.zeros((256, 128), F32)
    for j in range(9):
        gradient(j, 0)

    w = rope_back(acc[0:128] * SCORE_SCALE) * key_gain
    w_tan = rope_back(acc[128:256] * SCORE_SCALE) * key_gain
    xw = mean(lin * w)
    xw_tan = mean(tan * w) + mean(lin * w_tan)
    cot = (
        inv_tan * w
        + inv * w_tan
        - tan * (inv3 * xw)
        - lin * (3.0 * inv * inv * inv_tan * xw + inv3 * xw_tan)
    )
    cott[k] = jnp.transpose(cot).astype(BF16)
    cot_swap = rdma(cott.at[k], cott.at[k], one_s.at[2], one_r.at[2], other)
    cot_swap.start()
    drains.append(cot_swap.wait_send)
    cot_in = rdma(cott.at[1 - k], cott.at[1 - k], one_s.at[2], one_r.at[2], other)
    cot_in.wait_recv()
    cots = jnp.concatenate([cott[0], cott[1]], axis=1)

    def slice_of(yi):
        return pl.ds(pl.multiple_of(yi * 16, 16), 16)

    def rx_copy(dx, yi):
        cols = slice_of(yi)
        return rdma(
            ta.at[dx, cols], rx.at[dx - 1, cols], rx_s.at[dx - 1, yi], rx_r.at[dx - 1, yi], at_x((x + dx) % 4)
        )

    def sy_copy(dy):
        yi = (y + dy) % 8
        return rdma(tb.at[:, slice_of(yi)], sy.at[dy], sy_s.at[dy - 1], sy_r.at[dy - 1], at_y(yi))

    for dx in range(4):
        part = dot_nn(cots, nb[(x + dx) % 4])
        if dx:
            ta[dx] = part[:, 0:CUT].astype(BF16)
        else:
            py[...] = part
        tb[dx] = part[:, CUT:GROUP].astype(BF16)

    def rx_send(t, _):
        dy = far_step(t)
        sy_copy(dy).start()
        for dx in (2, 1, 3):
            rx_copy(dx, (y + dy) % 8).start()
        return 0

    lax.fori_loop(0, 7, rx_send, 0)
    for dx in (2, 1, 3):
        rx_copy(dx, y).start()

    def rx_drain(yi, _):
        for dx in (2, 1, 3):
            rx_copy(dx, yi).wait_send()
        return 0

    drains.append(lambda: lax.fori_loop(0, 8, rx_drain, 0))

    def rx_sum(yi):
        cols = slice_of(yi)
        total = py[cols, 0:CUT]
        for dx in (1, 3, 2):
            rx_copy(dx, yi).wait_recv()
            total = total + rx[dx - 1, cols, :].astype(F32)
        return total

    def ry_copy(dy):
        yi = (y + dy) % 8
        return rdma(ta.at[0, slice_of(yi)], ry.at[dy], ry_s.at[dy - 1], ry_r.at[dy - 1], at_y(yi))

    def y_sum(t, _):
        dy = far_step(t)
        yi = (y + dy) % 8
        ta[0, slice_of(yi), :] = rx_sum(yi).astype(BF16)
        ry_copy(dy).start()
        return 0

    lax.fori_loop(0, 7, y_sum, 0)

    def sy_wait(t, _):
        sy_copy(ring_step(t)).wait_recv()
        return 0

    lax.fori_loop(0, 7, sy_wait, 0)

    def sx_copy(dx):
        return rdma(sx.at[dx], sx.at[3 + dx], sx_s.at[dx - 1], sx_r.at[dx - 1], at_x((x + dx) % 4))

    for dx in (2, 1, 3, 0):
        part = tb[dx, slice_of(y), :].astype(F32) if dx else py[slice_of(y), CUT:GROUP]
        for dy in range(1, 8):
            part = part + sy[dy, dx].astype(F32)
        if dx:
            sx[dx] = part.astype(BF16)
            sx_copy(dx).start()
            drains.append(sx_copy(dx).wait_send)
    total_a = rx_sum(y)

    def ry_wait(t, _):
        ry_copy(ring_step(t)).wait_recv()
        return 0

    lax.fori_loop(0, 7, ry_wait, 0)
    for dy in range(1, 8):
        total_a = total_a + ry[dy].astype(F32)
    for dx in (1, 3, 2):
        sx_copy(dx).wait_recv()
        part = part + sx[3 + dx].astype(F32)
    total = jnp.concatenate([total_a, part], axis=1)

    def ry_drain(t, _):
        ry_copy(t + 1).wait_send()
        sy_copy(t + 1).wait_send()
        return 0

    drains.append(lambda: lax.fori_loop(0, 7, ry_drain, 0))

    def pz_copy(slot, src_z):
        zi = k * 4 + slot // 2
        return rdma(pz.at[slot], rz.at[src_z], rz_s.at[slot], rz_r.at[src_z], at_z(zi, slot % 2))

    for xi in range(4):

        @pl.when(x == xi)
        def _():
            tiles = placement(xi)[1]
            for slot in range(8):
                start = (slot // 2 * 672 + xi * 168) % 128 + slot % 2 * ROWS
                m, lead = start // 128, start % 128
                tile = tiles[slot // 2, m]
                piece = total[:, tile * 128 : tile * 128 + 128]
                if lead:
                    piece = pltpu.roll(piece, 128 - lead, 1)
                if lead + ROWS > 128:
                    tile = tiles[slot // 2, m + 1]
                    following = pltpu.roll(total[:, tile * 128 : tile * 128 + 128], 128 - lead, 1)
                    piece = jnp.where(lane128 < 128 - lead, piece, following)
                pz[slot] = jnp.where(lane128 < ROWS, piece, 0.0)

    def pz_self(slot):
        return jnp.logical_and(k * 4 + slot // 2 == z, slot % 2 == k)

    def pz_send(t, _):
        slot = (own_slot + 1 + t) % 8

        @pl.when(jnp.logical_not(pz_self(slot)))
        def _():
            pz_copy(slot, z).start()

        @pl.when(pz_self(slot))
        def _():
            rz[z] = pz[slot]

        return 0

    lax.fori_loop(0, 8, pz_send, 0)

    def pz_drain(slot, _):
        @pl.when(jnp.logical_not(pz_self(slot)))
        def _():
            pz_copy(slot, z).wait_send()

        return 0

    drains.append(lambda: lax.fori_loop(0, 8, pz_drain, 0))

    def rz_wait(t, _):
        src = (z + t) % 8

        @pl.when(jnp.logical_or(src != z, half != k))
        def _():
            pz_copy(0, src).wait_recv()

        return 0

    lax.fori_loop(0, 8, rz_wait, 0)
    product = rz[0]
    for src in range(1, 8):
        product = product + rz[src]
    product = product * D ** (-0.5)

    rows = [jnp.sum(bas[a] * product, axis=0, keepdims=True) for a in range(7)]
    rows.append(jnp.sum(product * product, axis=0, keepdims=True))
    sums = jnp.concatenate(rows + [gram], axis=0)

    def all_sum(stage, value, own, device):
        ar[stage, own] = value

        def copy(src, t, target):
            return rdma(
                ar.at[stage, src], ar.at[stage, src], ar_s.at[stage, t], ar_r.at[stage, src], device(target)
            )

        def send(t, _):
            copy(own, t, (own + far_step(t)) % 8).start()
            return 0

        lax.fori_loop(0, 7, send, 0)
        finish()

        def wait(t, _):
            copy((own + ring_step(t)) % 8, 0, own).wait_recv()
            return 0

        lax.fori_loop(0, 7, wait, 0)
        total = ar[stage, 0]
        for i in range(1, 8):
            total = total + ar[stage, i]

        def drain(t, _):
            copy(own, t, (own + far_step(t)) % 8).wait_send()
            return 0

        drains.append(lambda: lax.fori_loop(0, 7, drain, 0))
        return total

    sums = all_sum(0, sums, x * 2 + k, lambda i: (z * 8 + i, y))
    sums = all_sum(1, sums, z, lambda i: (i * 8 + x * 2 + k, y))
    sums = all_sum(2, sums, y, lambda i: (ctx, i))
    inner = jnp.sum(sums[0:8], axis=1, keepdims=True)
    coef = jnp.broadcast_to(inner / ENTRIES, (8, 128))
    coef_row = jnp.sum(jnp.where(jnp.logical_and(sub8 == lane8, sub8 < 7), coef, 0.0), axis=0, keepdims=True)
    quad = jnp.sum(coef_row * sums[8:16], axis=1, keepdims=True)
    norm = jnp.where(sub8 < 7, coef * (quad - 2.0 * inner), jnp.broadcast_to(inner, (8, 128)))
    squared = jnp.maximum(jnp.sum(norm, axis=0, keepdims=True), 0.0) / ENTRIES
    beta = jnp.sqrt(squared + EPSILON)
    residual = product
    for a in range(7):
        residual = residual - coef[a : a + 1] * bas[a]
    out[...] = (residual / beta)[:, 0:ROWS]
    coef_out[...] = coef_row[:, 0:7]
    beta_out[...] = beta[:, 0:1]

    finish()


def body(
    tokens,
    norm_gain,
    queries,
    values,
    upstream,
    segments,
    key_weight,
    key_gain,
    direction,
    stored_basis,
):
    dma = pltpu.SemaphoreType.DMA
    vmem = pl.BlockSpec(memory_space=pltpu.VMEM)
    out, coefficients, beta = pl.pallas_call(
        kernel,
        out_shape=tuple(jax.ShapeDtypeStruct(shape, F32) for shape in ((16, ROWS), (1, 7), (1, 1))),
        in_specs=[pl.BlockSpec(memory_space=pl.ANY)] + [vmem] * 10,
        out_specs=(vmem,) * 3,
        scratch_shapes=[
            pltpu.VMEM((128, D), BF16),
            pltpu.VMEM((2, 16, 128), BF16),
            pltpu.VMEM((7, 16, 128), F32),
            pltpu.VMEM((8, 16, 128), BF16),
            pltpu.VMEM((4, 2, 128, GROUP), BF16),
            pltpu.VMEM((4, 256, GROUP), BF16),
            pltpu.VMEM((4, 128, GROUP), BF16),
            pltpu.VMEM((9, 2, 128, 128), BF16),
            pltpu.VMEM((9, 8, 128), jnp.int32),
            pltpu.VMEM((2, 256, 128), F32),
            pltpu.VMEM((2, 128, 128), F32),
            pltpu.VMEM((9, 128, 128), F32),
            pltpu.VMEM((9, 128, 128), F32),
            pltpu.VMEM((9, 128, 128), F32),
            pltpu.VMEM((17, 9, 8, 128), F32),
            pltpu.VMEM((2, 128, 128), BF16),
            pltpu.VMEM((256, 128), F32),
            pltpu.VMEM((4, 128, CUT), BF16),
            pltpu.VMEM((4, 128, GROUP - CUT), BF16),
            pltpu.VMEM((3, 128, CUT), BF16),
            pltpu.VMEM((128, GROUP), F32),
            pltpu.VMEM((8, 16, CUT), BF16),
            pltpu.VMEM((8, 4, 16, GROUP - CUT), BF16),
            pltpu.VMEM((7, 16, GROUP - CUT), BF16),
            pltpu.VMEM((8, 16, 128), F32),
            pltpu.VMEM((8, 16, 128), F32),
            pltpu.VMEM((3, 8, 16, 128), F32),
            pltpu.VMEM((2, 128, 128), F32),
            dma((8,)),
            dma((8,)),
            dma((8,)),
            dma((8,)),
            dma((8,)),
            dma((8,)),
            dma((7,)),
            dma((8,)),
            dma((3, 8)),
            dma((4, 8)),
            dma((4, 8)),
            dma((4, 8)),
            dma((3,)),
            dma((3,)),
            dma,
            dma((16,)),
            dma((16,)),
            dma((3, 8)),
            dma((3, 8)),
            dma((7,)),
            dma((7,)),
            dma((7,)),
            dma((7,)),
            dma((3,)),
            dma((3,)),
            dma((8,)),
            dma((8,)),
            dma((3, 7)),
            dma((3, 8)),
        ],
        compiler_params=pltpu.CompilerParams(
            collective_id=0, has_side_effects=True, vmem_limit_bytes=56 * 2**20
        ),
        name="lanczos_step",
    )(
        tokens[0],
        norm_gain.reshape(D // 128, 128),
        queries[0],
        values[0],
        upstream[0],
        segments,
        key_weight.T,
        direction.T,
        key_gain[None],
        jnp.asarray(FREQS),
        jnp.swapaxes(stored_basis, 1, 2),
    )
    return coefficients.reshape(7), beta.reshape(()), out.T


def solution(mesh):
    in_specs = (
        P("dp", "ctx", None),
        P(),
        P("dp", "ctx", None),
        P("dp", "ctx", None),
        P("dp", "ctx", None),
        P("dp", "ctx"),
        P("ctx", "dp"),
        P(),
        P("ctx", "dp"),
        P(None, "ctx", "dp"),
    )
    out_specs = (P(), P(), P("ctx", "dp"))
    return jax.shard_map(body, mesh=mesh, in_specs=in_specs, out_specs=out_specs, check_vma=False)
```

```python
import jax
import jax.numpy as jnp
import numpy as np
from jax import lax
from jax.experimental import pallas as pl
from jax.experimental.pallas import tpu as pltpu
from jax.sharding import PartitionSpec as P

D = 5376
HD = 128
WINDOW = 1024
HALF = D // 2
ROWS = 84
SCORE_SCALE = 168.0 ** (-0.5)
EPSILON = 1e-06
ENTRIES = D * HD
GROUP = 768
CUT = 512
LOW = -1e30
MESH = pl.DeviceIdType.MESH
F32 = jnp.float32
BF16 = jnp.bfloat16
FREQS = np.tile(10000.0 ** (-np.arange(64) / 64.0), 2)[None].astype(np.float32)


def placement(xi):
    spans = {}
    for zi in range(4):
        start = (zi * 672 + xi * 168) % 128
        for m in range((start + 167) // 128 + 1):
            spans[zi, m] = (max(start - 128 * m, 0), min(start + 168 - 128 * m, 128))
    heads = sorted((span[1], key) for key, span in spans.items() if span[0] == 0 and span[1] < 128)
    tails = sorted((span[0], key) for key, span in spans.items() if span[0] > 0)
    tiles, free = {}, 0
    for end, key in reversed(heads):
        fits = [tail for tail in tails if tail[0] >= end]
        tiles[key] = free
        if fits:
            tails.remove(fits[0])
            tiles[fits[0][1]] = free
        free += 1
    for key in [tail[1] for tail in tails] + [key for key, span in spans.items() if span == (0, 128)]:
        tiles[key] = free
        free += 1
    return spans, tiles


def dot_nt(a, b):
    return lax.dot_general(a, b, (((1,), (1,)), ((), ())), preferred_element_type=F32)


def dot_nn(a, b):
    return lax.dot_general(a, b, (((1,), (0,)), ((), ())), preferred_element_type=F32)


def split(a):
    high = a.astype(BF16)
    return high, (a - high.astype(F32)).astype(BF16)


def ring_step(t):
    odd = t % 2
    return odd * (8 - (t + 1) // 2) + (1 - odd) * ((t + 2) // 2)


def far_step(t):
    return ring_step(6 - t)


def kernel(
    tok_in,
    gain_in,
    q_in,
    v_in,
    u_in,
    seg_in,
    w_in,
    dir_in,
    kg_in,
    freq_in,
    bas_in,
    out,
    coef_out,
    beta_out,
    tok,
    gain,
    v_own,
    seg_own,
    w_own,
    dir_own,
    kg,
    freq,
    bas_own,
    wt,
    bas,
    g1,
    wb,
    nb,
    ns,
    qu,
    segb,
    kl,
    klr,
    ev,
    sv,
    gv,
    rst,
    cott,
    acc,
    ta,
    tb,
    rx,
    py,
    ry,
    sy,
    sx,
    pz,
    rz,
    ar,
    cs,
    g1_s,
    g1_r,
    qu_s,
    qu_r,
    sg_s,
    sg_r,
    y_s,
    y_r,
    x_s,
    x_r,
    f_s,
    f_r,
    one_s,
    one_r,
    in_s,
    st_s,
    st_r,
    rx_s,
    rx_r,
    ry_s,
    ry_r,
    sy_s,
    sy_r,
    sx_s,
    sx_r,
    rz_s,
    rz_r,
    ar_s,
    ar_r,
):
    ctx = lax.axis_index("ctx")
    y = lax.axis_index("dp")
    z = ctx // 8
    x = (ctx // 2) % 4
    k = ctx % 2
    half = z // 4
    zz = z % 4
    parity = z % 2

    def at_z(zi, ki):
        return ((zi * 4 + x) * 2 + ki, y)

    def at_x(xi):
        return ((z * 4 + xi) * 2 + k, y)

    def at_y(yi):
        return (ctx, yi)

    def at_ctx(ci):
        return (ci % 64, y)

    other = ((z * 4 + x) * 2 + (1 - k), y)
    drains = []

    def finish():
        while drains:
            drains.pop()()


    def rdma(src, dst, send, recv, device):
        return pltpu.make_async_remote_copy(
            src_ref=src,
            dst_ref=dst,
            send_sem=send,
            recv_sem=recv,
            device_id=device,
            device_id_type=MESH,
        )

    barrier = pltpu.get_barrier_semaphore()

    def greet(device):
        pl.semaphore_signal(barrier, inc=1, device_id=device, device_id_type=MESH)

    for dz in (4, 3, 5, 2, 6):
        greet(at_z((z + dz) % 8, 0))
        greet(at_z((z + dz) % 8, 1))
    for dz in (1, 7):
        greet(at_z((z + dz) % 8, 1 - k))
    for dy in (4, 3, 5, 2, 6, 1, 7):
        greet(at_y((y + dy) % 8))
    for d in range(8, 0, -1):
        greet(at_ctx(ctx + d))
        greet(at_ctx(ctx + 64 - d))

    fetches = [
        pltpu.make_async_copy(source, target, in_s.at[i])
        for i, (source, target) in enumerate(
            (
                (w_in, w_own),
                (dir_in, dir_own),
                (q_in, qu.at[0, 0]),
                (u_in, qu.at[0, 1]),
                (seg_in, seg_own),
                (tok_in, tok),
                (gain_in, gain),
                (v_in, v_own),
                (kg_in, kg),
                (freq_in, freq),
                (bas_in, bas_own),
            )
        )
    ]
    for fetch in fetches:
        fetch.start()
    wt[...] = jnp.zeros((2, 16, 128), BF16)
    bas[...] = jnp.zeros((7, 16, 128), F32)
    for fetch in fetches[:2]:
        fetch.wait()
    wt[0, :, 0:ROWS] = w_own[...]
    wt[1, :, 0:ROWS] = (dir_own[...] * D ** (-0.5)).astype(BF16)
    pl.semaphore_wait(barrier, 35)

    own_slot = zz * 2 + k

    def g1_copy(zi, slot):
        return rdma(wt.at[zi % 2], g1.at[slot], g1_s.at[zi], g1_r.at[slot], at_z(zi, half))

    def g1_send(t, _):
        zi = (z + t) % 8

        @pl.when(jnp.logical_or(zi != z, half != k))
        def _():
            g1_copy(zi, own_slot).start()

        return 0

    lax.fori_loop(0, 8, g1_send, 0)

    def g1_drain(t, _):
        zi = (z + t) % 8

        @pl.when(jnp.logical_or(zi != z, half != k))
        def _():
            g1_copy(zi, own_slot).wait_send()

        return 0

    drains.append(lambda: lax.fori_loop(0, 8, g1_drain, 0))

    @pl.when(half == k)
    def _():
        g1[own_slot] = wt[parity]

    for fetch in fetches[2:]:
        fetch.wait()
    segb[0] = jnp.broadcast_to(seg_own[...], (8, 128))

    def qu_far():
        return [
            rdma(ref.at[0], ref.at[8], sends.at[7], recvs.at[7], at_ctx(ctx + 56))
            for ref, sends, recvs in ((qu, qu_s, qu_r), (segb, sg_s, sg_r))
        ]

    def qu_pair(source, j, device):
        return [
            rdma(ref.at[source], ref.at[j], sends.at[j - 1], recvs.at[j - 1], device)
            for ref, sends, recvs in ((qu, qu_s, qu_r), (segb, sg_s, sg_r))
        ]

    def qu_chip(dx):
        return qu_pair(8 * (1 - (x + dx) // 4), 8 - 2 * dx, at_x((x + dx) % 4))

    def qu_core():
        return qu_pair(8 * (1 - k), 7 - 6 * k, other)

    def qu_next(dx):
        return qu_pair(8 - 2 * dx, 7 - 2 * dx + 2 * k, other)

    for copy in qu_far():
        copy.start()
        drains.append(copy.wait_send)

    lane128 = lax.broadcasted_iota(jnp.int32, (1, 128), 1)
    gain_tiles = gain[...].astype(F32)
    gain_row = jnp.concatenate([gain_tiles[i : i + 1] for i in range(D // 128)], axis=1)

    def norm_chunk(r):
        rows = pl.ds(pl.multiple_of(r * 16, 16), 16)
        floats = tok[rows, :].astype(F32)
        scale = lax.rsqrt(jnp.mean(floats * floats, axis=-1, keepdims=True) + EPSILON)
        normed = floats * scale * gain_row
        for hh in range(2):
            for xi in range(4):
                spans, tiles = placement(xi)
                columns = [None] * 6
                for key, (low, high) in spans.items():
                    source = (hh * HALF + key[0] * 672 + xi * 168) // 128 + key[1]
                    part = normed[:, source * 128 : source * 128 + 128]
                    held = columns[tiles[key]]
                    if held is not None:
                        part = jnp.where(lane128 < high, part, held) if low == 0 else jnp.where(lane128 >= low, part, held)
                    columns[tiles[key]] = part
                group = jnp.concatenate(columns, axis=1).astype(BF16)

                @pl.when(k == hh)
                def _():
                    nb[xi, pl.ds(pl.multiple_of(k * 128 + r * 16, 16), 16), :] = group

                @pl.when(k != hh)
                def _():
                    ns[xi, rows, :] = group


    def norm(r, _):
        norm_chunk(r)
        return 0

    lax.fori_loop(0, 8, norm, 0)
    swap = rdma(
        ns, nb.at[:, pl.ds(pl.multiple_of(k * 128, 128), 128), :], one_s.at[0], one_r.at[0], other
    )
    swap.start()
    drains.append(swap.wait_send)


    def g1_wait(slot, _):
        zi = half * 0 + k * 4 + slot // 2
        mine = jnp.logical_and(zi == z, slot % 2 == k)

        @pl.when(jnp.logical_not(mine))
        def _():
            g1_copy(z, slot).wait_recv()

        return 0

    lax.fori_loop(0, 8, g1_wait, 0)
    for xi in range(4):

        @pl.when(x == xi)
        def _():
            tiles = placement(xi)[1]
            columns = [jnp.zeros((16, 128), F32) for _ in range(6)]
            for slot in range(8):
                piece = g1[slot].astype(F32)
                start = (slot // 2 * 672 + xi * 168) % 128 + slot % 2 * ROWS
                m, lead = start // 128, start % 128
                moved = pltpu.roll(piece, lead, 1) if lead else piece
                tile = tiles[slot // 2, m]
                columns[tile] = columns[tile] + jnp.where(lane128 >= lead, moved, 0.0)
                if lead + ROWS > 128:
                    tile = tiles[slot // 2, m + 1]
                    columns[tile] = columns[tile] + jnp.where(lane128 < lead, moved, 0.0)
            own = pl.ds(pl.multiple_of(y * 16, 16), 16)
            wb[xi, parity, own, :] = jnp.concatenate(columns, axis=1).astype(BF16)

    def piece_at(matrix, xi, yi):
        return wb.at[xi, matrix, pl.ds(pl.multiple_of(yi * 16, 16), 16), :]

    def y_copy(src_y, dst_y, t):
        piece = piece_at(parity, x, src_y)
        return rdma(piece, piece, y_s.at[t], y_r.at[src_y], at_y(dst_y))

    def x_copy(src_x, yi, dst_x, t):
        piece = piece_at(parity, src_x, yi)
        return rdma(piece, piece, x_s.at[t, yi], x_r.at[src_x, yi], at_x(dst_x))

    def f_copy(matrix, xi, yi):
        piece = piece_at(matrix, xi, yi)
        target = at_z((z + 1 + 6 * (yi % 2)) % 8, k)
        return rdma(piece, piece, f_s.at[xi, yi], f_r.at[xi, yi], target)

    def y_send(t, _):
        y_copy(y, (y + far_step(t)) % 8, t).start()
        return 0

    lax.fori_loop(0, 7, y_send, 0)

    def y_drain(t, _):
        y_copy(y, (y + far_step(t)) % 8, t).wait_send()
        return 0

    drains.append(lambda: lax.fori_loop(0, 7, y_drain, 0))

    def x_send(yi):
        for t, dx in enumerate((2, 1, 3)):
            x_copy(x, yi, (x + dx) % 4, t).start()
        f_copy(parity, x, yi).start()

    x_send(y)
    lane = lax.broadcasted_iota(jnp.int32, (128, 128), 1)
    sub = lax.broadcasted_iota(jnp.int32, (128, 128), 0)
    angle = (ctx * 128 + sub).astype(F32) * freq[...]
    cs[0] = jnp.cos(angle)
    cs[1] = jnp.sin(angle) * jnp.where(lane < 64, -1.0, 1.0)
    key_doc = jnp.transpose(jnp.broadcast_to(segb[0, 0:1].astype(F32), (128, 128)))

    def y_forward(t, _):
        src = (y + ring_step(t)) % 8
        y_copy(src, y, 0).wait_recv()
        x_send(src)
        return 0

    lax.fori_loop(0, 7, y_forward, 0)

    def x_drain(yi, _):
        for t, dx in enumerate((2, 1, 3)):
            x_copy(x, yi, (x + dx) % 4, t).wait_send()
        for xi in range(4):
            f_copy(parity, xi, yi).wait_send()
        return 0

    drains.append(lambda: lax.fori_loop(0, 8, x_drain, 0))

    def x_forward(t, _):
        yi = (y + ring_step(t - 1)) % 8
        for dx in (1, 3, 2):
            xi = (x + dx) % 4
            x_copy(xi, yi, x, 0).wait_recv()
            f_copy(parity, xi, yi).start()
        return 0

    lax.fori_loop(0, 8, x_forward, 0)

    for copy in qu_far():
        copy.wait_recv()

    for dx in (2, 1, 3):
        for copy in qu_chip(dx):
            copy.start()
            drains.append(copy.wait_send)
    for copy in qu_core():
        copy.start()
        drains.append(copy.wait_send)

    swap.wait_recv()
    first = jnp.zeros((256, 128), F32)
    for xi in range(4):
        first = first + dot_nt(nb[xi], wb[xi, parity])
    kl[parity] = first
    second = jnp.zeros((256, 128), F32)
    for xi in range(4):

        def f_wait(yi, _):
            f_copy(1 - parity, xi, yi).wait_recv()
            return 0

        lax.fori_loop(0, 8, f_wait, 0)
        second = second + dot_nt(nb[xi], wb[xi, 1 - parity])
    kl[1 - parity] = second
    mine = pl.ds(pl.multiple_of(k * 128, 128), 128)
    theirs = pl.ds(pl.multiple_of((1 - k) * 128, 128), 128)
    kl_swap = rdma(kl.at[:, theirs], klr, one_s.at[1], one_r.at[1], other)
    kl_swap.start()
    drains.append(kl_swap.wait_send)
    for dx in (1, 3, 2):
        for copy in qu_chip(dx):
            copy.wait_recv()
        for copy in qu_next(dx):
            copy.start()
            drains.append(copy.wait_send)

    for j in range(1, 8, 2):
        for copy in qu_pair(0, j, other):
            copy.wait_recv()
    kl_swap.wait_recv()
    lin, tan = kl[0, mine] + klr[0], kl[1, mine] + klr[1]
    cosine, sine = cs[0], cs[1]
    key_gain = kg[...]

    def rope(vec):
        return vec * cosine + pltpu.roll(vec, 64, 1) * sine

    def rope_back(vec):
        return vec * cosine - pltpu.roll(vec, 64, 1) * sine

    def mean(vec):
        return jnp.mean(vec, axis=-1, keepdims=True)

    inv = lax.rsqrt(mean(lin * lin) + EPSILON)
    inv3 = inv * inv * inv
    inv_tan = -inv3 * mean(lin * tan)
    keyed = rope(lin * inv * key_gain) * SCORE_SCALE
    keyed_tan = rope((tan * inv + lin * inv_tan) * key_gain) * SCORE_SCALE
    k_high, k_low = split(keyed)
    t_high, t_low = split(keyed_tan)
    stacked_keys = jnp.concatenate([k_high, k_low, t_high, t_low], axis=0)
    value_rows = v_own[...]

    def score(j, _):
        raw = dot_nt(stacked_keys, qu[j, 0])
        s = raw[0:128] + raw[128:256]
        st = raw[256:384] + raw[384:512]
        g = dot_nt(value_rows, qu[j, 1])
        gap = 128 * j + lane - sub
        near = jnp.logical_and(gap >= 0, gap < WINDOW)
        same = key_doc == segb[j, 0:1].astype(F32)
        allowed = jnp.logical_and(jnp.logical_and(near, same), ctx + j < 64)
        top = jnp.max(jnp.where(allowed, s, LOW), axis=0, keepdims=True)
        e = jnp.where(allowed, jnp.exp(s - top), 0.0)
        est = e * st
        rows = [top] + [jnp.sum(m, axis=0, keepdims=True) for m in (e, e * g, est, est * g)]
        rst[8, j] = jnp.concatenate(rows + [jnp.zeros((3, 128), F32)], axis=0)
        ev[j] = e
        sv[j] = st
        gv[j] = g
        return 0

    for j in range(9):
        score(j, 0)

    def st_copies():
        copies = []
        for d in (8, 7, 6, 5, 4, 3, 2, 1):
            n = 9 - d
            copies.append(
                rdma(
                    rst.at[8, pl.ds(d, n)],
                    rst.at[8 + d, pl.ds(0, n)],
                    st_s.at[d - 1],
                    st_r.at[d - 1],
                    at_ctx(ctx + d),
                )
            )
            copies.append(
                rdma(
                    rst.at[8, pl.ds(0, n)],
                    rst.at[8 - d, pl.ds(d, n)],
                    st_s.at[7 + d],
                    st_r.at[7 + d],
                    at_ctx(ctx + 64 - d),
                )
            )
        return copies

    st_list = st_copies()
    for copy in st_list:
        copy.start()
        drains.append(copy.wait_send)
    finish()
    for copy in st_list:
        copy.wait_recv()

    def gradient(j, _):
        stats = [rst[8 - j + t, j] for t in range(9)]
        peak = stats[0][0:1]
        for stat in stats[1:]:
            peak = jnp.maximum(peak, stat[0:1])
        total = jnp.zeros((8, 128), F32)
        for stat in stats:
            total = total + jnp.exp(stat[0:1] - peak) * stat
        filled = total[1:2] > 0.0
        scale = jnp.where(filled, 1.0 / jnp.where(filled, total[1:2], 1.0), 0.0)
        m = total[2:3] * scale
        a = total[3:4] * scale
        m_tan = total[4:5] * scale - a * m
        p = ev[j] * (jnp.exp(rst[8, j][0:1] - peak) * scale)
        rest = gv[j] - m
        ds = p * rest
        ds_tan = p * ((sv[j] - a) * rest - m_tan)
        high, low = split(jnp.concatenate([ds, ds_tan], axis=0))
        prod = dot_nn(jnp.concatenate([high, low], axis=0), qu[j, 0])
        acc[...] += prod[0:256] + prod[256:512]
        return 0

    acc[...] = jnp.zeros((256, 128), F32)
    for j in range(9):
        gradient(j, 0)

    w = rope_back(acc[0:128] * SCORE_SCALE) * key_gain
    w_tan = rope_back(acc[128:256] * SCORE_SCALE) * key_gain
    xw = mean(lin * w)
    xw_tan = mean(tan * w) + mean(lin * w_tan)
    cot = (
        inv_tan * w
        + inv * w_tan
        - tan * (inv3 * xw)
        - lin * (3.0 * inv * inv * inv_tan * xw + inv3 * xw_tan)
    )
    cott[k] = jnp.transpose(cot).astype(BF16)
    cot_swap = rdma(cott.at[k], cott.at[k], one_s.at[2], one_r.at[2], other)
    cot_swap.start()
    drains.append(cot_swap.wait_send)
    cot_in = rdma(cott.at[1 - k], cott.at[1 - k], one_s.at[2], one_r.at[2], other)
    cot_in.wait_recv()
    cots = jnp.concatenate([cott[0], cott[1]], axis=1)

    def slice_of(yi):
        return pl.ds(pl.multiple_of(yi * 16, 16), 16)

    def rx_copy(dx, yi):
        cols = slice_of(yi)
        return rdma(
            ta.at[dx, cols], rx.at[dx - 1, cols], rx_s.at[dx - 1, yi], rx_r.at[dx - 1, yi], at_x((x + dx) % 4)
        )

    def sy_copy(dy):
        yi = (y + dy) % 8
        return rdma(tb.at[:, slice_of(yi)], sy.at[dy], sy_s.at[dy - 1], sy_r.at[dy - 1], at_y(yi))

    for dx in range(4):
        part = dot_nn(cots, nb[(x + dx) % 4])
        if dx:
            ta[dx] = part[:, 0:CUT].astype(BF16)
        else:
            py[...] = part
        tb[dx] = part[:, CUT:GROUP].astype(BF16)

    def rx_send(t, _):
        dy = far_step(t)
        sy_copy(dy).start()
        for dx in (2, 1, 3):
            rx_copy(dx, (y + dy) % 8).start()
        return 0

    lax.fori_loop(0, 7, rx_send, 0)
    for dx in (2, 1, 3):
        rx_copy(dx, y).start()

    def rx_drain(yi, _):
        for dx in (2, 1, 3):
            rx_copy(dx, yi).wait_send()
        return 0

    drains.append(lambda: lax.fori_loop(0, 8, rx_drain, 0))

    bas[0:6, :, 0:ROWS] = bas_own[...]
    bas[6, :, 0:ROWS] = dir_own[...]
    lane8 = lax.broadcasted_iota(jnp.int32, (8, 128), 1)
    sub8 = lax.broadcasted_iota(jnp.int32, (8, 128), 0)
    gram = jnp.zeros((8, 128), F32)
    for a in range(7):
        for b in range(a, 7):
            dotted = jnp.sum(jnp.sum(bas[a] * bas[b], axis=0, keepdims=True), axis=1, keepdims=True)
            spot = jnp.logical_and(sub8 == a, lane8 == 64 + b)
            if a != b:
                spot = jnp.logical_or(spot, jnp.logical_and(sub8 == b, lane8 == 64 + a))
            gram = jnp.where(spot, dotted, gram)

    def rx_sum(yi):
        cols = slice_of(yi)
        total = py[cols, 0:CUT]
        for dx in (1, 3, 2):
            rx_copy(dx, yi).wait_recv()
            total = total + rx[dx - 1, cols, :].astype(F32)
        return total

    def ry_copy(dy):
        yi = (y + dy) % 8
        return rdma(ta.at[0, slice_of(yi)], ry.at[dy], ry_s.at[dy - 1], ry_r.at[dy - 1], at_y(yi))

    def y_sum(t, _):
        dy = far_step(t)
        yi = (y + dy) % 8
        ta[0, slice_of(yi), :] = rx_sum(yi).astype(BF16)
        ry_copy(dy).start()
        return 0

    lax.fori_loop(0, 7, y_sum, 0)

    def sy_wait(t, _):
        sy_copy(ring_step(t)).wait_recv()
        return 0

    lax.fori_loop(0, 7, sy_wait, 0)

    def sx_copy(dx):
        return rdma(sx.at[dx], sx.at[3 + dx], sx_s.at[dx - 1], sx_r.at[dx - 1], at_x((x + dx) % 4))

    for dx in (2, 1, 3, 0):
        part = tb[dx, slice_of(y), :].astype(F32) if dx else py[slice_of(y), CUT:GROUP]
        for dy in range(1, 8):
            part = part + sy[dy, dx].astype(F32)
        if dx:
            sx[dx] = part.astype(BF16)
            sx_copy(dx).start()
            drains.append(sx_copy(dx).wait_send)
    total_a = rx_sum(y)

    def ry_wait(t, _):
        ry_copy(ring_step(t)).wait_recv()
        return 0

    lax.fori_loop(0, 7, ry_wait, 0)
    for dy in range(1, 8):
        total_a = total_a + ry[dy].astype(F32)
    for dx in (1, 3, 2):
        sx_copy(dx).wait_recv()
        part = part + sx[3 + dx].astype(F32)
    total = jnp.concatenate([total_a, part], axis=1)

    def ry_drain(t, _):
        ry_copy(t + 1).wait_send()
        sy_copy(t + 1).wait_send()
        return 0

    drains.append(lambda: lax.fori_loop(0, 7, ry_drain, 0))

    def pz_copy(slot, src_z):
        zi = k * 4 + slot // 2
        return rdma(pz.at[slot], rz.at[src_z], rz_s.at[slot], rz_r.at[src_z], at_z(zi, slot % 2))

    for xi in range(4):

        @pl.when(x == xi)
        def _():
            tiles = placement(xi)[1]
            for slot in range(8):
                start = (slot // 2 * 672 + xi * 168) % 128 + slot % 2 * ROWS
                m, lead = start // 128, start % 128
                tile = tiles[slot // 2, m]
                piece = total[:, tile * 128 : tile * 128 + 128]
                if lead:
                    piece = pltpu.roll(piece, 128 - lead, 1)
                if lead + ROWS > 128:
                    tile = tiles[slot // 2, m + 1]
                    following = pltpu.roll(total[:, tile * 128 : tile * 128 + 128], 128 - lead, 1)
                    piece = jnp.where(lane128 < 128 - lead, piece, following)
                pz[slot] = jnp.where(lane128 < ROWS, piece, 0.0)

    def pz_self(slot):
        return jnp.logical_and(k * 4 + slot // 2 == z, slot % 2 == k)

    def pz_send(t, _):
        slot = (own_slot + 1 + t) % 8

        @pl.when(jnp.logical_not(pz_self(slot)))
        def _():
            pz_copy(slot, z).start()

        @pl.when(pz_self(slot))
        def _():
            rz[z] = pz[slot]

        return 0

    lax.fori_loop(0, 8, pz_send, 0)

    def pz_drain(slot, _):
        @pl.when(jnp.logical_not(pz_self(slot)))
        def _():
            pz_copy(slot, z).wait_send()

        return 0

    drains.append(lambda: lax.fori_loop(0, 8, pz_drain, 0))

    def rz_wait(t, _):
        src = (z + t) % 8

        @pl.when(jnp.logical_or(src != z, half != k))
        def _():
            pz_copy(0, src).wait_recv()

        return 0

    lax.fori_loop(0, 8, rz_wait, 0)
    product = rz[0]
    for src in range(1, 8):
        product = product + rz[src]
    product = product * D ** (-0.5)

    rows = [jnp.sum(bas[a] * product, axis=0, keepdims=True) for a in range(7)]
    rows.append(jnp.sum(product * product, axis=0, keepdims=True))
    sums = jnp.concatenate(rows, axis=0)
    sums = jnp.where(lane8 < 64, sums + pltpu.roll(sums, 64, 1), gram)

    def all_sum(stage, value, own, device):
        ar[stage, own] = value

        def copy(src, t, target):
            return rdma(
                ar.at[stage, src], ar.at[stage, src], ar_s.at[stage, t], ar_r.at[stage, src], device(target)
            )

        def send(t, _):
            copy(own, t, (own + far_step(t)) % 8).start()
            return 0

        lax.fori_loop(0, 7, send, 0)
        finish()

        def wait(t, _):
            copy((own + ring_step(t)) % 8, 0, own).wait_recv()
            return 0

        lax.fori_loop(0, 7, wait, 0)
        total = ar[stage, 0]
        for i in range(1, 8):
            total = total + ar[stage, i]

        def drain(t, _):
            copy(own, t, (own + far_step(t)) % 8).wait_send()
            return 0

        drains.append(lambda: lax.fori_loop(0, 7, drain, 0))
        return total

    sums = all_sum(0, sums, x * 2 + k, lambda i: (z * 8 + i, y))
    sums = all_sum(1, sums, z, lambda i: (i * 8 + x * 2 + k, y))
    sums = all_sum(2, sums, y, lambda i: (ctx, i))
    inner = jnp.sum(jnp.where(lane8 < 64, sums, 0.0), axis=1, keepdims=True)
    coef = jnp.broadcast_to(inner / ENTRIES, (8, 128))
    spots = jnp.logical_and(sub8 == lane8 % 64, sub8 < 7)
    coef_row = jnp.sum(jnp.where(spots, coef, 0.0), axis=0, keepdims=True)
    quad = jnp.sum(jnp.where(lane8 < 64, 0.0, coef_row * sums), axis=1, keepdims=True)
    norm = jnp.where(sub8 < 7, coef * (quad - 2.0 * inner), jnp.broadcast_to(inner, (8, 128)))
    squared = jnp.maximum(jnp.sum(norm, axis=0, keepdims=True), 0.0) / ENTRIES
    beta = jnp.sqrt(squared + EPSILON)
    residual = product
    for a in range(7):
        residual = residual - coef[a : a + 1] * bas[a]
    out[...] = (residual / beta)[:, 0:ROWS]
    coef_out[...] = coef_row[:, 0:7]
    beta_out[...] = beta[:, 0:1]

    finish()


def hand_over(coef_in, beta_in, next_in, coef_out, beta_out, next_out):
    coef_out[...] = coef_in[...]
    beta_out[...] = beta_in[...]
    next_out[...] = next_in[...]


def body(
    tokens,
    norm_gain,
    queries,
    values,
    upstream,
    segments,
    key_weight,
    key_gain,
    direction,
    stored_basis,
):
    dma = pltpu.SemaphoreType.DMA
    vmem = pl.BlockSpec(memory_space=pltpu.VMEM)
    out, coefficients, beta = pl.pallas_call(
        kernel,
        out_shape=tuple(jax.ShapeDtypeStruct(shape, F32) for shape in ((16, ROWS), (1, 7), (1, 1))),
        in_specs=[pl.BlockSpec(memory_space=pl.ANY)] * 11,
        out_specs=(vmem,) * 3,
        scratch_shapes=[
            pltpu.VMEM((128, D), BF16),
            pltpu.VMEM((D // 128, 128), BF16),
            pltpu.VMEM((128, 128), BF16),
            pltpu.VMEM((1, 128), jnp.int32),
            pltpu.VMEM((16, ROWS), BF16),
            pltpu.VMEM((16, ROWS), F32),
            pltpu.VMEM((1, 128), F32),
            pltpu.VMEM((1, 128), F32),
            pltpu.VMEM((6, 16, ROWS), F32),
            pltpu.VMEM((2, 16, 128), BF16),
            pltpu.VMEM((7, 16, 128), F32),
            pltpu.VMEM((8, 16, 128), BF16),
            pltpu.VMEM((4, 2, 128, GROUP), BF16),
            pltpu.VMEM((4, 256, GROUP), BF16),
            pltpu.VMEM((4, 128, GROUP), BF16),
            pltpu.VMEM((9, 2, 128, 128), BF16),
            pltpu.VMEM((9, 8, 128), jnp.int32),
            pltpu.VMEM((2, 256, 128), F32),
            pltpu.VMEM((2, 128, 128), F32),
            pltpu.VMEM((9, 128, 128), F32),
            pltpu.VMEM((9, 128, 128), F32),
            pltpu.VMEM((9, 128, 128), F32),
            pltpu.VMEM((17, 9, 8, 128), F32),
            pltpu.VMEM((2, 128, 128), BF16),
            pltpu.VMEM((256, 128), F32),
            pltpu.VMEM((4, 128, CUT), BF16),
            pltpu.VMEM((4, 128, GROUP - CUT), BF16),
            pltpu.VMEM((3, 128, CUT), BF16),
            pltpu.VMEM((128, GROUP), F32),
            pltpu.VMEM((8, 16, CUT), BF16),
            pltpu.VMEM((8, 4, 16, GROUP - CUT), BF16),
            pltpu.VMEM((7, 16, GROUP - CUT), BF16),
            pltpu.VMEM((8, 16, 128), F32),
            pltpu.VMEM((8, 16, 128), F32),
            pltpu.VMEM((3, 8, 8, 128), F32),
            pltpu.VMEM((2, 128, 128), F32),
            dma((8,)),
            dma((8,)),
            dma((8,)),
            dma((8,)),
            dma((8,)),
            dma((8,)),
            dma((7,)),
            dma((8,)),
            dma((3, 8)),
            dma((4, 8)),
            dma((4, 8)),
            dma((4, 8)),
            dma((3,)),
            dma((3,)),
            dma((11,)),
            dma((16,)),
            dma((16,)),
            dma((3, 8)),
            dma((3, 8)),
            dma((7,)),
            dma((7,)),
            dma((7,)),
            dma((7,)),
            dma((3,)),
            dma((3,)),
            dma((8,)),
            dma((8,)),
            dma((3, 7)),
            dma((3, 8)),
        ],
        compiler_params=pltpu.CompilerParams(
            collective_id=0, has_side_effects=True, vmem_limit_bytes=56 * 2**20
        ),
        name="lanczos_step",
    )(
        tokens[0],
        norm_gain.reshape(D // 128, 128),
        queries[0],
        values[0],
        upstream[0],
        segments,
        key_weight.T,
        direction.T,
        key_gain[None],
        jnp.asarray(FREQS),
        jnp.swapaxes(stored_basis, 1, 2),
    )
    coefficients, beta, out = pl.pallas_call(
        hand_over,
        out_shape=tuple(jax.ShapeDtypeStruct(shape, F32) for shape in ((1, 7), (1, 1), (16, ROWS))),
        in_specs=[vmem] * 3,
        out_specs=(vmem,) * 3,
        name="hand_over",
    )(coefficients, beta, out)
    return coefficients.reshape(7), beta.reshape(()), out.T


def solution(mesh):
    in_specs = (
        P("dp", "ctx", None),
        P(),
        P("dp", "ctx", None),
        P("dp", "ctx", None),
        P("dp", "ctx", None),
        P("dp", "ctx"),
        P("ctx", "dp"),
        P(),
        P("ctx", "dp"),
        P(None, "ctx", "dp"),
    )
    out_specs = (P(), P(), P("ctx", "dp"))
    return jax.shard_map(body, mesh=mesh, in_specs=in_specs, out_specs=out_specs, check_vma=False)
```

```python
import jax
import jax.numpy as jnp
import numpy as np
from jax import lax
from jax.experimental import pallas as pl
from jax.experimental.pallas import tpu as pltpu
from jax.sharding import PartitionSpec as P

D = 5376
HD = 128
WINDOW = 1024
HALF = D // 2
ROWS = 84
SCORE_SCALE = 168.0 ** (-0.5)
EPSILON = 1e-06
ENTRIES = D * HD
GROUP = 768
CUT = 512
LOW = -1e30
MESH = pl.DeviceIdType.MESH
F32 = jnp.float32
BF16 = jnp.bfloat16
FREQS = np.tile(10000.0 ** (-np.arange(64) / 64.0), 2)[None].astype(np.float32)


def placement(xi):
    spans = {}
    for zi in range(4):
        start = (zi * 672 + xi * 168) % 128
        for m in range((start + 167) // 128 + 1):
            spans[zi, m] = (max(start - 128 * m, 0), min(start + 168 - 128 * m, 128))
    heads = sorted((span[1], key) for key, span in spans.items() if span[0] == 0 and span[1] < 128)
    tails = sorted((span[0], key) for key, span in spans.items() if span[0] > 0)
    tiles, free = {}, 0
    for end, key in reversed(heads):
        fits = [tail for tail in tails if tail[0] >= end]
        tiles[key] = free
        if fits:
            tails.remove(fits[0])
            tiles[fits[0][1]] = free
        free += 1
    for key in [tail[1] for tail in tails] + [key for key, span in spans.items() if span == (0, 128)]:
        tiles[key] = free
        free += 1
    return spans, tiles


def dot_nt(a, b):
    return lax.dot_general(a, b, (((1,), (1,)), ((), ())), preferred_element_type=F32)


def dot_nn(a, b):
    return lax.dot_general(a, b, (((1,), (0,)), ((), ())), preferred_element_type=F32)


def split(a):
    high = a.astype(BF16)
    return high, (a - high.astype(F32)).astype(BF16)


def unrolled(start, end, step):
    for t in range(start, end):
        step(t, 0)


def ring_step(t):
    odd = t % 2
    return odd * (8 - (t + 1) // 2) + (1 - odd) * ((t + 2) // 2)


def far_step(t):
    return ring_step(6 - t)


def kernel(
    tok_in,
    gain_in,
    q_in,
    v_in,
    u_in,
    seg_in,
    w_in,
    dir_in,
    kg_in,
    freq_in,
    bas_in,
    out,
    coef_out,
    beta_out,
    tok,
    gain,
    v_own,
    seg_own,
    w_own,
    dir_own,
    kg,
    freq,
    bas_own,
    wt,
    bas,
    g1,
    wb,
    nb,
    ns,
    qu,
    segb,
    kl,
    klr,
    ev,
    sv,
    gv,
    rst,
    cott,
    acc,
    ta,
    tb,
    rx,
    py,
    ry,
    sy,
    sx,
    pz,
    rz,
    ar,
    cs,
    g1_s,
    g1_r,
    qu_s,
    qu_r,
    sg_s,
    sg_r,
    y_s,
    y_r,
    x_s,
    x_r,
    f_s,
    f_r,
    one_s,
    one_r,
    in_s,
    st_s,
    st_r,
    rx_s,
    rx_r,
    ry_s,
    ry_r,
    sy_s,
    sy_r,
    sx_s,
    sx_r,
    rz_s,
    rz_r,
    ar_s,
    ar_r,
):
    ctx = lax.axis_index("ctx")
    y = lax.axis_index("dp")
    z = ctx // 8
    x = (ctx // 2) % 4
    k = ctx % 2
    half = z // 4
    zz = z % 4
    parity = z % 2

    def at_z(zi, ki):
        return ((zi * 4 + x) * 2 + ki, y)

    def at_x(xi):
        return ((z * 4 + xi) * 2 + k, y)

    def at_y(yi):
        return (ctx, yi)

    def at_ctx(ci):
        return (ci % 64, y)

    other = ((z * 4 + x) * 2 + (1 - k), y)
    drains = []

    def finish():
        while drains:
            drains.pop()()


    def rdma(src, dst, send, recv, device):
        return pltpu.make_async_remote_copy(
            src_ref=src,
            dst_ref=dst,
            send_sem=send,
            recv_sem=recv,
            device_id=device,
            device_id_type=MESH,
        )

    barrier = pltpu.get_barrier_semaphore()

    def greet(device):
        pl.semaphore_signal(barrier, inc=1, device_id=device, device_id_type=MESH)

    for dz in (4, 3, 5, 2, 6):
        greet(at_z((z + dz) % 8, 0))
        greet(at_z((z + dz) % 8, 1))
    for dz in (1, 7):
        greet(at_z((z + dz) % 8, 1 - k))
    for dy in (4, 3, 5, 2, 6, 1, 7):
        greet(at_y((y + dy) % 8))
    for d in range(8, 0, -1):
        greet(at_ctx(ctx + d))
        greet(at_ctx(ctx + 64 - d))

    fetches = [
        pltpu.make_async_copy(source, target, in_s.at[i])
        for i, (source, target) in enumerate(
            (
                (w_in, w_own),
                (dir_in, dir_own),
                (q_in, qu.at[0, 0]),
                (u_in, qu.at[0, 1]),
                (seg_in, seg_own),
                (tok_in, tok),
                (gain_in, gain),
                (v_in, v_own),
                (kg_in, kg),
                (freq_in, freq),
                (bas_in, bas_own),
            )
        )
    ]
    for fetch in fetches:
        fetch.start()
    wt[...] = jnp.zeros((2, 16, 128), BF16)
    bas[...] = jnp.zeros((7, 16, 128), F32)
    for fetch in fetches[:2]:
        fetch.wait()
    wt[0, :, 0:ROWS] = w_own[...]
    wt[1, :, 0:ROWS] = (dir_own[...] * D ** (-0.5)).astype(BF16)
    pl.semaphore_wait(barrier, 35)

    own_slot = zz * 2 + k

    def g1_copy(zi, slot):
        return rdma(wt.at[zi % 2], g1.at[slot], g1_s.at[zi], g1_r.at[slot], at_z(zi, half))

    def g1_send(t, _):
        zi = (z + t) % 8

        @pl.when(jnp.logical_or(zi != z, half != k))
        def _():
            g1_copy(zi, own_slot).start()

        return 0

    unrolled(0, 8, g1_send)

    def g1_drain(t, _):
        zi = (z + t) % 8

        @pl.when(jnp.logical_or(zi != z, half != k))
        def _():
            g1_copy(zi, own_slot).wait_send()

        return 0

    drains.append(lambda: unrolled(0, 8, g1_drain))

    @pl.when(half == k)
    def _():
        g1[own_slot] = wt[parity]

    for fetch in fetches[2:]:
        fetch.wait()
    segb[0] = jnp.broadcast_to(seg_own[...], (8, 128))

    def qu_far():
        return [
            rdma(ref.at[0], ref.at[8], sends.at[7], recvs.at[7], at_ctx(ctx + 56))
            for ref, sends, recvs in ((qu, qu_s, qu_r), (segb, sg_s, sg_r))
        ]

    def qu_pair(source, j, device):
        return [
            rdma(ref.at[source], ref.at[j], sends.at[j - 1], recvs.at[j - 1], device)
            for ref, sends, recvs in ((qu, qu_s, qu_r), (segb, sg_s, sg_r))
        ]

    def qu_chip(dx):
        return qu_pair(8 * (1 - (x + dx) // 4), 8 - 2 * dx, at_x((x + dx) % 4))

    def qu_core():
        return qu_pair(8 * (1 - k), 7 - 6 * k, other)

    def qu_next(dx):
        return qu_pair(8 - 2 * dx, 7 - 2 * dx + 2 * k, other)

    for copy in qu_far():
        copy.start()
        drains.append(copy.wait_send)

    lane128 = lax.broadcasted_iota(jnp.int32, (1, 128), 1)
    gain_tiles = gain[...].astype(F32)
    gain_row = jnp.concatenate([gain_tiles[i : i + 1] for i in range(D // 128)], axis=1)

    def norm_chunk(r):
        rows = pl.ds(pl.multiple_of(r * 16, 16), 16)
        floats = tok[rows, :].astype(F32)
        scale = lax.rsqrt(jnp.mean(floats * floats, axis=-1, keepdims=True) + EPSILON)
        normed = floats * scale * gain_row
        for hh in range(2):
            for xi in range(4):
                spans, tiles = placement(xi)
                columns = [None] * 6
                for key, (low, high) in spans.items():
                    source = (hh * HALF + key[0] * 672 + xi * 168) // 128 + key[1]
                    part = normed[:, source * 128 : source * 128 + 128]
                    held = columns[tiles[key]]
                    if held is not None:
                        part = jnp.where(lane128 < high, part, held) if low == 0 else jnp.where(lane128 >= low, part, held)
                    columns[tiles[key]] = part
                group = jnp.concatenate(columns, axis=1).astype(BF16)

                @pl.when(k == hh)
                def _():
                    nb[xi, pl.ds(pl.multiple_of(k * 128 + r * 16, 16), 16), :] = group

                @pl.when(k != hh)
                def _():
                    ns[xi, rows, :] = group


    def norm(r, _):
        norm_chunk(r)
        return 0

    lax.fori_loop(0, 8, norm, 0)
    swap = rdma(
        ns, nb.at[:, pl.ds(pl.multiple_of(k * 128, 128), 128), :], one_s.at[0], one_r.at[0], other
    )
    swap.start()
    drains.append(swap.wait_send)


    def g1_wait(slot, _):
        zi = half * 0 + k * 4 + slot // 2
        mine = jnp.logical_and(zi == z, slot % 2 == k)

        @pl.when(jnp.logical_not(mine))
        def _():
            g1_copy(z, slot).wait_recv()

        return 0

    unrolled(0, 8, g1_wait)
    for xi in range(4):

        @pl.when(x == xi)
        def _():
            tiles = placement(xi)[1]
            columns = [jnp.zeros((16, 128), F32) for _ in range(6)]
            for slot in range(8):
                piece = g1[slot].astype(F32)
                start = (slot // 2 * 672 + xi * 168) % 128 + slot % 2 * ROWS
                m, lead = start // 128, start % 128
                moved = pltpu.roll(piece, lead, 1) if lead else piece
                tile = tiles[slot // 2, m]
                columns[tile] = columns[tile] + jnp.where(lane128 >= lead, moved, 0.0)
                if lead + ROWS > 128:
                    tile = tiles[slot // 2, m + 1]
                    columns[tile] = columns[tile] + jnp.where(lane128 < lead, moved, 0.0)
            own = pl.ds(pl.multiple_of(y * 16, 16), 16)
            wb[xi, parity, own, :] = jnp.concatenate(columns, axis=1).astype(BF16)

    def piece_at(matrix, xi, yi):
        return wb.at[xi, matrix, pl.ds(pl.multiple_of(yi * 16, 16), 16), :]

    def y_copy(src_y, dst_y, t):
        piece = piece_at(parity, x, src_y)
        return rdma(piece, piece, y_s.at[t], y_r.at[src_y], at_y(dst_y))

    def x_copy(src_x, yi, dst_x, t):
        piece = piece_at(parity, src_x, yi)
        return rdma(piece, piece, x_s.at[t, yi], x_r.at[src_x, yi], at_x(dst_x))

    def f_copy(matrix, xi, yi):
        piece = piece_at(matrix, xi, yi)
        target = at_z((z + 1 + 6 * (yi % 2)) % 8, k)
        return rdma(piece, piece, f_s.at[xi, yi], f_r.at[xi, yi], target)

    def y_send(t, _):
        y_copy(y, (y + far_step(t)) % 8, t).start()
        return 0

    unrolled(0, 7, y_send)

    def y_drain(t, _):
        y_copy(y, (y + far_step(t)) % 8, t).wait_send()
        return 0

    drains.append(lambda: unrolled(0, 7, y_drain))

    def x_send(yi):
        for t, dx in enumerate((2, 1, 3)):
            x_copy(x, yi, (x + dx) % 4, t).start()
        f_copy(parity, x, yi).start()

    x_send(y)
    lane = lax.broadcasted_iota(jnp.int32, (128, 128), 1)
    sub = lax.broadcasted_iota(jnp.int32, (128, 128), 0)
    angle = (ctx * 128 + sub).astype(F32) * freq[...]
    cs[0] = jnp.cos(angle)
    cs[1] = jnp.sin(angle) * jnp.where(lane < 64, -1.0, 1.0)
    key_doc = jnp.transpose(jnp.broadcast_to(segb[0, 0:1].astype(F32), (128, 128)))

    def y_forward(t, _):
        src = (y + ring_step(t)) % 8
        y_copy(src, y, 0).wait_recv()
        x_send(src)
        return 0

    unrolled(0, 7, y_forward)

    def x_drain(yi, _):
        for t, dx in enumerate((2, 1, 3)):
            x_copy(x, yi, (x + dx) % 4, t).wait_send()
        for xi in range(4):
            f_copy(parity, xi, yi).wait_send()
        return 0

    drains.append(lambda: unrolled(0, 8, x_drain))

    def x_forward(t, _):
        yi = (y + ring_step(t - 1)) % 8
        for dx in (1, 3, 2):
            xi = (x + dx) % 4
            x_copy(xi, yi, x, 0).wait_recv()
            f_copy(parity, xi, yi).start()
        return 0

    unrolled(0, 8, x_forward)

    for copy in qu_far():
        copy.wait_recv()

    for dx in (2, 1, 3):
        for copy in qu_chip(dx):
            copy.start()
            drains.append(copy.wait_send)
    for copy in qu_core():
        copy.start()
        drains.append(copy.wait_send)

    swap.wait_recv()
    first = jnp.zeros((256, 128), F32)
    for xi in range(4):
        first = first + dot_nt(nb[xi], wb[xi, parity])
    kl[parity] = first
    second = jnp.zeros((256, 128), F32)
    for xi in range(4):

        def f_wait(yi, _):
            f_copy(1 - parity, xi, yi).wait_recv()
            return 0

        unrolled(0, 8, f_wait)
        second = second + dot_nt(nb[xi], wb[xi, 1 - parity])
    kl[1 - parity] = second
    mine = pl.ds(pl.multiple_of(k * 128, 128), 128)
    theirs = pl.ds(pl.multiple_of((1 - k) * 128, 128), 128)
    kl_swap = rdma(kl.at[:, theirs], klr, one_s.at[1], one_r.at[1], other)
    kl_swap.start()
    drains.append(kl_swap.wait_send)
    for dx in (1, 3, 2):
        for copy in qu_chip(dx):
            copy.wait_recv()
        for copy in qu_next(dx):
            copy.start()
            drains.append(copy.wait_send)

    for j in range(1, 8, 2):
        for copy in qu_pair(0, j, other):
            copy.wait_recv()
    kl_swap.wait_recv()
    lin, tan = kl[0, mine] + klr[0], kl[1, mine] + klr[1]
    cosine, sine = cs[0], cs[1]
    key_gain = kg[...]

    def rope(vec):
        return vec * cosine + pltpu.roll(vec, 64, 1) * sine

    def rope_back(vec):
        return vec * cosine - pltpu.roll(vec, 64, 1) * sine

    def mean(vec):
        return jnp.mean(vec, axis=-1, keepdims=True)

    inv = lax.rsqrt(mean(lin * lin) + EPSILON)
    inv3 = inv * inv * inv
    inv_tan = -inv3 * mean(lin * tan)
    keyed = rope(lin * inv * key_gain) * SCORE_SCALE
    keyed_tan = rope((tan * inv + lin * inv_tan) * key_gain) * SCORE_SCALE
    k_high, k_low = split(keyed)
    t_high, t_low = split(keyed_tan)
    stacked_keys = jnp.concatenate([k_high, k_low, t_high, t_low], axis=0)
    value_rows = v_own[...]

    def score(j, _):
        raw = dot_nt(stacked_keys, qu[j, 0])
        s = raw[0:128] + raw[128:256]
        st = raw[256:384] + raw[384:512]
        g = dot_nt(value_rows, qu[j, 1])
        gap = 128 * j + lane - sub
        near = jnp.logical_and(gap >= 0, gap < WINDOW)
        same = key_doc == segb[j, 0:1].astype(F32)
        allowed = jnp.logical_and(jnp.logical_and(near, same), ctx + j < 64)
        top = jnp.max(jnp.where(allowed, s, LOW), axis=0, keepdims=True)
        e = jnp.where(allowed, jnp.exp(s - top), 0.0)
        est = e * st
        rows = [top] + [jnp.sum(m, axis=0, keepdims=True) for m in (e, e * g, est, est * g)]
        rst[8, j] = jnp.concatenate(rows + [jnp.zeros((3, 128), F32)], axis=0)
        ev[j] = e
        sv[j] = st
        gv[j] = g
        return 0

    for j in range(9):
        score(j, 0)

    def st_copies():
        copies = []
        for d in (8, 7, 6, 5, 4, 3, 2, 1):
            n = 9 - d
            copies.append(
                rdma(
                    rst.at[8, pl.ds(d, n)],
                    rst.at[8 + d, pl.ds(0, n)],
                    st_s.at[d - 1],
                    st_r.at[d - 1],
                    at_ctx(ctx + d),
                )
            )
            copies.append(
                rdma(
                    rst.at[8, pl.ds(0, n)],
                    rst.at[8 - d, pl.ds(d, n)],
                    st_s.at[7 + d],
                    st_r.at[7 + d],
                    at_ctx(ctx + 64 - d),
                )
            )
        return copies

    st_list = st_copies()
    for copy in st_list:
        copy.start()
        drains.append(copy.wait_send)
    finish()
    for copy in st_list:
        copy.wait_recv()

    def gradient(j, _):
        stats = [rst[8 - j + t, j] for t in range(9)]
        peak = stats[0][0:1]
        for stat in stats[1:]:
            peak = jnp.maximum(peak, stat[0:1])
        total = jnp.zeros((8, 128), F32)
        for stat in stats:
            total = total + jnp.exp(stat[0:1] - peak) * stat
        filled = total[1:2] > 0.0
        scale = jnp.where(filled, 1.0 / jnp.where(filled, total[1:2], 1.0), 0.0)
        m = total[2:3] * scale
        a = total[3:4] * scale
        m_tan = total[4:5] * scale - a * m
        p = ev[j] * (jnp.exp(rst[8, j][0:1] - peak) * scale)
        rest = gv[j] - m
        ds = p * rest
        ds_tan = p * ((sv[j] - a) * rest - m_tan)
        high, low = split(jnp.concatenate([ds, ds_tan], axis=0))
        prod = dot_nn(jnp.concatenate([high, low], axis=0), qu[j, 0])
        acc[...] += prod[0:256] + prod[256:512]
        return 0

    acc[...] = jnp.zeros((256, 128), F32)
    for j in range(9):
        gradient(j, 0)

    w = rope_back(acc[0:128] * SCORE_SCALE) * key_gain
    w_tan = rope_back(acc[128:256] * SCORE_SCALE) * key_gain
    xw = mean(lin * w)
    xw_tan = mean(tan * w) + mean(lin * w_tan)
    cot = (
        inv_tan * w
        + inv * w_tan
        - tan * (inv3 * xw)
        - lin * (3.0 * inv * inv * inv_tan * xw + inv3 * xw_tan)
    )
    cott[k] = jnp.transpose(cot).astype(BF16)
    cot_swap = rdma(cott.at[k], cott.at[k], one_s.at[2], one_r.at[2], other)
    cot_swap.start()
    drains.append(cot_swap.wait_send)
    cot_in = rdma(cott.at[1 - k], cott.at[1 - k], one_s.at[2], one_r.at[2], other)
    cot_in.wait_recv()
    cots = jnp.concatenate([cott[0], cott[1]], axis=1)

    def slice_of(yi):
        return pl.ds(pl.multiple_of(yi * 16, 16), 16)

    def rx_copy(dx, yi):
        cols = slice_of(yi)
        return rdma(
            ta.at[dx, cols], rx.at[dx - 1, cols], rx_s.at[dx - 1, yi], rx_r.at[dx - 1, yi], at_x((x + dx) % 4)
        )

    def sy_copy(dy):
        yi = (y + dy) % 8
        return rdma(tb.at[:, slice_of(yi)], sy.at[dy], sy_s.at[dy - 1], sy_r.at[dy - 1], at_y(yi))

    for dx in range(4):
        part = dot_nn(cots, nb[(x + dx) % 4, :, CUT:GROUP])
        tb[dx] = part.astype(BF16)
        if dx == 0:
            py[:, CUT:GROUP] = part

    def sy_send(t, _):
        sy_copy(far_step(t)).start()
        return 0

    unrolled(0, 7, sy_send)
    for dx in (2, 1, 3):
        ta[dx] = dot_nn(cots, nb[(x + dx) % 4, :, 0:CUT]).astype(BF16)

    def rx_send(t, _):
        for dx in (2, 1, 3):
            rx_copy(dx, (y + far_step(t)) % 8).start()
        return 0

    unrolled(0, 8, rx_send)
    py[:, 0:CUT] = dot_nn(cots, nb[x, :, 0:CUT])

    def rx_drain(yi, _):
        for dx in (2, 1, 3):
            rx_copy(dx, yi).wait_send()
        return 0

    drains.append(lambda: unrolled(0, 8, rx_drain))

    bas[0:6, :, 0:ROWS] = bas_own[...]
    bas[6, :, 0:ROWS] = dir_own[...]
    lane8 = lax.broadcasted_iota(jnp.int32, (8, 128), 1)
    sub8 = lax.broadcasted_iota(jnp.int32, (8, 128), 0)
    gram = jnp.zeros((8, 128), F32)
    for a in range(7):
        for b in range(a, 7):
            dotted = jnp.sum(jnp.sum(bas[a] * bas[b], axis=0, keepdims=True), axis=1, keepdims=True)
            spot = jnp.logical_and(sub8 == a, lane8 == 64 + b)
            if a != b:
                spot = jnp.logical_or(spot, jnp.logical_and(sub8 == b, lane8 == 64 + a))
            gram = jnp.where(spot, dotted, gram)

    def rx_sum(yi):
        cols = slice_of(yi)
        total = py[cols, 0:CUT]
        for dx in (1, 3, 2):
            rx_copy(dx, yi).wait_recv()
            total = total + rx[dx - 1, cols, :].astype(F32)
        return total

    def ry_copy(dy):
        yi = (y + dy) % 8
        return rdma(ta.at[0, slice_of(yi)], ry.at[dy], ry_s.at[dy - 1], ry_r.at[dy - 1], at_y(yi))

    def y_sum(t, _):
        dy = far_step(t)
        yi = (y + dy) % 8
        ta[0, slice_of(yi), :] = rx_sum(yi).astype(BF16)
        ry_copy(dy).start()
        return 0

    unrolled(0, 7, y_sum)

    def sy_wait(t, _):
        sy_copy(ring_step(t)).wait_recv()
        return 0

    unrolled(0, 7, sy_wait)

    def sx_copy(dx):
        return rdma(sx.at[dx], sx.at[3 + dx], sx_s.at[dx - 1], sx_r.at[dx - 1], at_x((x + dx) % 4))

    for dx in (2, 1, 3, 0):
        part = tb[dx, slice_of(y), :].astype(F32) if dx else py[slice_of(y), CUT:GROUP]
        for dy in range(1, 8):
            part = part + sy[dy, dx].astype(F32)
        if dx:
            sx[dx] = part.astype(BF16)
            sx_copy(dx).start()
            drains.append(sx_copy(dx).wait_send)
    total_a = rx_sum(y)

    def ry_wait(t, _):
        ry_copy(ring_step(t)).wait_recv()
        return 0

    unrolled(0, 7, ry_wait)
    for dy in range(1, 8):
        total_a = total_a + ry[dy].astype(F32)
    for dx in (1, 3, 2):
        sx_copy(dx).wait_recv()
        part = part + sx[3 + dx].astype(F32)
    total = jnp.concatenate([total_a, part], axis=1)

    def ry_drain(t, _):
        ry_copy(t + 1).wait_send()
        sy_copy(t + 1).wait_send()
        return 0

    drains.append(lambda: unrolled(0, 7, ry_drain))

    def pz_copy(slot, src_z):
        zi = k * 4 + slot // 2
        return rdma(pz.at[slot], rz.at[src_z], rz_s.at[slot], rz_r.at[src_z], at_z(zi, slot % 2))

    for xi in range(4):

        @pl.when(x == xi)
        def _():
            tiles = placement(xi)[1]
            for slot in range(8):
                start = (slot // 2 * 672 + xi * 168) % 128 + slot % 2 * ROWS
                m, lead = start // 128, start % 128
                tile = tiles[slot // 2, m]
                piece = total[:, tile * 128 : tile * 128 + 128]
                if lead:
                    piece = pltpu.roll(piece, 128 - lead, 1)
                if lead + ROWS > 128:
                    tile = tiles[slot // 2, m + 1]
                    following = pltpu.roll(total[:, tile * 128 : tile * 128 + 128], 128 - lead, 1)
                    piece = jnp.where(lane128 < 128 - lead, piece, following)
                pz[slot] = jnp.where(lane128 < ROWS, piece, 0.0)

    def pz_self(slot):
        return jnp.logical_and(k * 4 + slot // 2 == z, slot % 2 == k)

    def pz_send(t, _):
        slot = (own_slot + 1 + t) % 8

        @pl.when(jnp.logical_not(pz_self(slot)))
        def _():
            pz_copy(slot, z).start()

        @pl.when(pz_self(slot))
        def _():
            rz[z] = pz[slot]

        return 0

    unrolled(0, 8, pz_send)

    def pz_drain(slot, _):
        @pl.when(jnp.logical_not(pz_self(slot)))
        def _():
            pz_copy(slot, z).wait_send()

        return 0

    drains.append(lambda: unrolled(0, 8, pz_drain))

    def rz_wait(t, _):
        src = (z + t) % 8

        @pl.when(jnp.logical_or(src != z, half != k))
        def _():
            pz_copy(0, src).wait_recv()

        return 0

    unrolled(0, 8, rz_wait)
    product = rz[0]
    for src in range(1, 8):
        product = product + rz[src]
    product = product * D ** (-0.5)

    rows = [jnp.sum(bas[a] * product, axis=0, keepdims=True) for a in range(7)]
    rows.append(jnp.sum(product * product, axis=0, keepdims=True))
    sums = jnp.concatenate(rows, axis=0)
    sums = jnp.where(lane8 < 64, sums + pltpu.roll(sums, 64, 1), gram)

    def all_sum(stage, value, own, device):
        ar[stage, own] = value

        def copy(src, t, target):
            return rdma(
                ar.at[stage, src], ar.at[stage, src], ar_s.at[stage, t], ar_r.at[stage, src], device(target)
            )

        def send(t, _):
            copy(own, t, (own + far_step(t)) % 8).start()
            return 0

        unrolled(0, 7, send)
        finish()

        def wait(t, _):
            copy((own + ring_step(t)) % 8, 0, own).wait_recv()
            return 0

        unrolled(0, 7, wait)
        total = ar[stage, 0]
        for i in range(1, 8):
            total = total + ar[stage, i]

        def drain(t, _):
            copy(own, t, (own + far_step(t)) % 8).wait_send()
            return 0

        drains.append(lambda: unrolled(0, 7, drain))
        return total

    sums = all_sum(0, sums, x * 2 + k, lambda i: (z * 8 + i, y))
    sums = all_sum(1, sums, z, lambda i: (i * 8 + x * 2 + k, y))
    sums = all_sum(2, sums, y, lambda i: (ctx, i))
    inner = jnp.sum(jnp.where(lane8 < 64, sums, 0.0), axis=1, keepdims=True)
    coef = jnp.broadcast_to(inner / ENTRIES, (8, 128))
    spots = jnp.logical_and(sub8 == lane8 % 64, sub8 < 7)
    coef_row = jnp.sum(jnp.where(spots, coef, 0.0), axis=0, keepdims=True)
    quad = jnp.sum(jnp.where(lane8 < 64, 0.0, coef_row * sums), axis=1, keepdims=True)
    norm = jnp.where(sub8 < 7, coef * (quad - 2.0 * inner), jnp.broadcast_to(inner, (8, 128)))
    squared = jnp.maximum(jnp.sum(norm, axis=0, keepdims=True), 0.0) / ENTRIES
    beta = jnp.sqrt(squared + EPSILON)
    residual = product
    for a in range(7):
        residual = residual - coef[a : a + 1] * bas[a]
    out[...] = (residual / beta)[:, 0:ROWS]
    coef_out[...] = coef_row[:, 0:7]
    beta_out[...] = beta[:, 0:1]

    finish()


def hand_over(coef_in, beta_in, next_in, coef_out, beta_out, next_out):
    coef_out[...] = coef_in[...]
    beta_out[...] = beta_in[...]
    next_out[...] = next_in[...]


def body(
    tokens,
    norm_gain,
    queries,
    values,
    upstream,
    segments,
    key_weight,
    key_gain,
    direction,
    stored_basis,
):
    dma = pltpu.SemaphoreType.DMA
    vmem = pl.BlockSpec(memory_space=pltpu.VMEM)
    out, coefficients, beta = pl.pallas_call(
        kernel,
        out_shape=tuple(jax.ShapeDtypeStruct(shape, F32) for shape in ((16, ROWS), (1, 7), (1, 1))),
        in_specs=[pl.BlockSpec(memory_space=pl.ANY)] * 11,
        out_specs=(vmem,) * 3,
        scratch_shapes=[
            pltpu.VMEM((128, D), BF16),
            pltpu.VMEM((D // 128, 128), BF16),
            pltpu.VMEM((128, 128), BF16),
            pltpu.VMEM((1, 128), jnp.int32),
            pltpu.VMEM((16, ROWS), BF16),
            pltpu.VMEM((16, ROWS), F32),
            pltpu.VMEM((1, 128), F32),
            pltpu.VMEM((1, 128), F32),
            pltpu.VMEM((6, 16, ROWS), F32),
            pltpu.VMEM((2, 16, 128), BF16),
            pltpu.VMEM((7, 16, 128), F32),
            pltpu.VMEM((8, 16, 128), BF16),
            pltpu.VMEM((4, 2, 128, GROUP), BF16),
            pltpu.VMEM((4, 256, GROUP), BF16),
            pltpu.VMEM((4, 128, GROUP), BF16),
            pltpu.VMEM((9, 2, 128, 128), BF16),
            pltpu.VMEM((9, 8, 128), jnp.int32),
            pltpu.VMEM((2, 256, 128), F32),
            pltpu.VMEM((2, 128, 128), F32),
            pltpu.VMEM((9, 128, 128), F32),
            pltpu.VMEM((9, 128, 128), F32),
            pltpu.VMEM((9, 128, 128), F32),
            pltpu.VMEM((17, 9, 8, 128), F32),
            pltpu.VMEM((2, 128, 128), BF16),
            pltpu.VMEM((256, 128), F32),
            pltpu.VMEM((4, 128, CUT), BF16),
            pltpu.VMEM((4, 128, GROUP - CUT), BF16),
            pltpu.VMEM((3, 128, CUT), BF16),
            pltpu.VMEM((128, GROUP), F32),
            pltpu.VMEM((8, 16, CUT), BF16),
            pltpu.VMEM((8, 4, 16, GROUP - CUT), BF16),
            pltpu.VMEM((7, 16, GROUP - CUT), BF16),
            pltpu.VMEM((8, 16, 128), F32),
            pltpu.VMEM((8, 16, 128), F32),
            pltpu.VMEM((3, 8, 8, 128), F32),
            pltpu.VMEM((2, 128, 128), F32),
            dma((8,)),
            dma((8,)),
            dma((8,)),
            dma((8,)),
            dma((8,)),
            dma((8,)),
            dma((7,)),
            dma((8,)),
            dma((3, 8)),
            dma((4, 8)),
            dma((4, 8)),
            dma((4, 8)),
            dma((3,)),
            dma((3,)),
            dma((11,)),
            dma((16,)),
            dma((16,)),
            dma((3, 8)),
            dma((3, 8)),
            dma((7,)),
            dma((7,)),
            dma((7,)),
            dma((7,)),
            dma((3,)),
            dma((3,)),
            dma((8,)),
            dma((8,)),
            dma((3, 7)),
            dma((3, 8)),
        ],
        compiler_params=pltpu.CompilerParams(
            collective_id=0, has_side_effects=True, vmem_limit_bytes=56 * 2**20
        ),
        name="lanczos_step",
    )(
        tokens[0],
        norm_gain.reshape(D // 128, 128),
        queries[0],
        values[0],
        upstream[0],
        segments,
        key_weight.T,
        direction.T,
        key_gain[None],
        jnp.asarray(FREQS),
        jnp.swapaxes(stored_basis, 1, 2),
    )
    coefficients, beta, out = pl.pallas_call(
        hand_over,
        out_shape=tuple(jax.ShapeDtypeStruct(shape, F32) for shape in ((1, 7), (1, 1), (16, ROWS))),
        in_specs=[vmem] * 3,
        out_specs=(vmem,) * 3,
        name="hand_over",
    )(coefficients, beta, out)
    return coefficients.reshape(7), beta.reshape(()), out.T


def solution(mesh):
    in_specs = (
        P("dp", "ctx", None),
        P(),
        P("dp", "ctx", None),
        P("dp", "ctx", None),
        P("dp", "ctx", None),
        P("dp", "ctx"),
        P("ctx", "dp"),
        P(),
        P("ctx", "dp"),
        P(None, "ctx", "dp"),
    )
    out_specs = (P(), P(), P("ctx", "dp"))
    return jax.shard_map(body, mesh=mesh, in_specs=in_specs, out_specs=out_specs, check_vma=False)
```

```python
import jax
import jax.numpy as jnp
import numpy as np
from jax import lax
from jax.experimental import pallas as pl
from jax.experimental.pallas import tpu as pltpu
from jax.sharding import PartitionSpec as P

D = 5376
HD = 128
WINDOW = 1024
HALF = D // 2
ROWS = 84
SCORE_SCALE = 168.0 ** (-0.5)
EPSILON = 1e-06
ENTRIES = D * HD
GROUP = 768
CUT = 512
LOW = -1e30
MESH = pl.DeviceIdType.MESH
F32 = jnp.float32
BF16 = jnp.bfloat16
FREQS = np.tile(10000.0 ** (-np.arange(64) / 64.0), 2)[None].astype(np.float32)


def placement(xi):
    spans = {}
    for zi in range(4):
        start = (zi * 672 + xi * 168) % 128
        for m in range((start + 167) // 128 + 1):
            spans[zi, m] = (max(start - 128 * m, 0), min(start + 168 - 128 * m, 128))
    heads = sorted((span[1], key) for key, span in spans.items() if span[0] == 0 and span[1] < 128)
    tails = sorted((span[0], key) for key, span in spans.items() if span[0] > 0)
    tiles, free = {}, 0
    for end, key in reversed(heads):
        fits = [tail for tail in tails if tail[0] >= end]
        tiles[key] = free
        if fits:
            tails.remove(fits[0])
            tiles[fits[0][1]] = free
        free += 1
    for key in [tail[1] for tail in tails] + [key for key, span in spans.items() if span == (0, 128)]:
        tiles[key] = free
        free += 1
    return spans, tiles


def dot_nt(a, b):
    return lax.dot_general(a, b, (((1,), (1,)), ((), ())), preferred_element_type=F32)


def dot_nn(a, b):
    return lax.dot_general(a, b, (((1,), (0,)), ((), ())), preferred_element_type=F32)


def split(a):
    high = a.astype(BF16)
    return high, (a - high.astype(F32)).astype(BF16)


def unrolled(start, end, step):
    for t in range(start, end):
        step(t, 0)


def ring_step(t):
    odd = t % 2
    return odd * (8 - (t + 1) // 2) + (1 - odd) * ((t + 2) // 2)


def far_step(t):
    return ring_step(6 - t)


def kernel(
    tok_in,
    gain_in,
    q_in,
    v_in,
    u_in,
    seg_in,
    w_in,
    dir_in,
    kg_in,
    freq_in,
    bas_in,
    out,
    coef_out,
    beta_out,
    tok,
    gain,
    v_own,
    seg_own,
    w_own,
    dir_own,
    kg,
    freq,
    bas_own,
    wt,
    bas,
    g1,
    wb,
    nb,
    ns,
    qu,
    segb,
    kl,
    klr,
    ev,
    sv,
    gv,
    rst,
    cott,
    acc,
    ta,
    tb,
    rx,
    py,
    ry,
    sy,
    sx,
    pz,
    rz,
    ar,
    cs,
    g1_s,
    g1_r,
    qu_s,
    qu_r,
    sg_s,
    sg_r,
    y_s,
    y_r,
    x_s,
    x_r,
    f_s,
    f_r,
    one_s,
    one_r,
    in_s,
    st_s,
    st_r,
    rx_s,
    rx_r,
    ry_s,
    ry_r,
    sy_s,
    sy_r,
    sx_s,
    sx_r,
    rz_s,
    rz_r,
    ar_s,
    ar_r,
):
    ctx = lax.axis_index("ctx")
    y = lax.axis_index("dp")
    z = ctx // 8
    x = (ctx // 2) % 4
    k = ctx % 2
    half = z // 4
    zz = z % 4
    parity = z % 2

    def at_z(zi, ki):
        return ((zi * 4 + x) * 2 + ki, y)

    def at_x(xi):
        return ((z * 4 + xi) * 2 + k, y)

    def at_y(yi):
        return (ctx, yi)

    def at_ctx(ci):
        return (ci % 64, y)

    other = ((z * 4 + x) * 2 + (1 - k), y)
    drains = []

    def finish():
        while drains:
            drains.pop()()


    def rdma(src, dst, send, recv, device):
        return pltpu.make_async_remote_copy(
            src_ref=src,
            dst_ref=dst,
            send_sem=send,
            recv_sem=recv,
            device_id=device,
            device_id_type=MESH,
        )

    barrier = pltpu.get_barrier_semaphore()

    def greet(device):
        pl.semaphore_signal(barrier, inc=1, device_id=device, device_id_type=MESH)

    for dz in (4, 3, 5, 2, 6):
        greet(at_z((z + dz) % 8, 0))
        greet(at_z((z + dz) % 8, 1))
    for dz in (1, 7):
        greet(at_z((z + dz) % 8, 1 - k))
    for dy in (4, 3, 5, 2, 6, 1, 7):
        greet(at_y((y + dy) % 8))
    for d in range(8, 0, -1):
        greet(at_ctx(ctx + d))
        greet(at_ctx(ctx + 64 - d))

    fetches = [
        pltpu.make_async_copy(source, target, in_s.at[i])
        for i, (source, target) in enumerate(
            (
                (w_in, w_own),
                (dir_in, dir_own),
                (q_in, qu.at[0, 0]),
                (u_in, qu.at[0, 1]),
                (seg_in, seg_own),
                (tok_in, tok),
                (gain_in, gain),
                (v_in, v_own),
                (kg_in, kg),
                (freq_in, freq),
                (bas_in, bas_own),
            )
        )
    ]
    for fetch in fetches:
        fetch.start()
    wt[...] = jnp.zeros((2, 16, 128), BF16)
    bas[...] = jnp.zeros((7, 16, 128), F32)
    for fetch in fetches[:2]:
        fetch.wait()
    wt[0, :, 0:ROWS] = w_own[...]
    wt[1, :, 0:ROWS] = (dir_own[...] * D ** (-0.5)).astype(BF16)
    pl.semaphore_wait(barrier, 35)

    own_slot = zz * 2 + k

    def g1_copy(zi, slot):
        return rdma(wt.at[zi % 2], g1.at[slot], g1_s.at[zi], g1_r.at[slot], at_z(zi, half))

    def g1_send(t, _):
        zi = (z + t) % 8

        @pl.when(jnp.logical_or(zi != z, half != k))
        def _():
            g1_copy(zi, own_slot).start()

        return 0

    unrolled(0, 8, g1_send)

    def g1_drain(t, _):
        zi = (z + t) % 8

        @pl.when(jnp.logical_or(zi != z, half != k))
        def _():
            g1_copy(zi, own_slot).wait_send()

        return 0

    drains.append(lambda: unrolled(0, 8, g1_drain))

    @pl.when(half == k)
    def _():
        g1[own_slot] = wt[parity]

    for fetch in fetches[2:]:
        fetch.wait()
    segb[0] = jnp.broadcast_to(seg_own[...], (8, 128))

    def qu_far():
        return [
            rdma(ref.at[0], ref.at[8], sends.at[7], recvs.at[7], at_ctx(ctx + 56))
            for ref, sends, recvs in ((qu, qu_s, qu_r), (segb, sg_s, sg_r))
        ]

    def qu_pair(source, j, device):
        return [
            rdma(ref.at[source], ref.at[j], sends.at[j - 1], recvs.at[j - 1], device)
            for ref, sends, recvs in ((qu, qu_s, qu_r), (segb, sg_s, sg_r))
        ]

    def qu_chip(dx):
        return qu_pair(8 * (1 - (x + dx) // 4), 8 - 2 * dx, at_x((x + dx) % 4))

    def qu_core():
        return qu_pair(8 * (1 - k), 7 - 6 * k, other)

    def qu_next(dx):
        return qu_pair(8 - 2 * dx, 7 - 2 * dx + 2 * k, other)

    for copy in qu_far():
        copy.start()
        drains.append(copy.wait_send)

    lane128 = lax.broadcasted_iota(jnp.int32, (1, 128), 1)
    gain_tiles = gain[...].astype(F32)
    gain_row = jnp.concatenate([gain_tiles[i : i + 1] for i in range(D // 128)], axis=1)

    def norm_chunk(r):
        rows = pl.ds(pl.multiple_of(r * 16, 16), 16)
        floats = tok[rows, :].astype(F32)
        scale = lax.rsqrt(jnp.mean(floats * floats, axis=-1, keepdims=True) + EPSILON)
        normed = floats * scale * gain_row
        for hh in range(2):
            for xi in range(4):
                spans, tiles = placement(xi)
                columns = [None] * 6
                for key, (low, high) in spans.items():
                    source = (hh * HALF + key[0] * 672 + xi * 168) // 128 + key[1]
                    part = normed[:, source * 128 : source * 128 + 128]
                    held = columns[tiles[key]]
                    if held is not None:
                        part = jnp.where(lane128 < high, part, held) if low == 0 else jnp.where(lane128 >= low, part, held)
                    columns[tiles[key]] = part
                group = jnp.concatenate(columns, axis=1).astype(BF16)

                @pl.when(k == hh)
                def _():
                    nb[xi, pl.ds(pl.multiple_of(k * 128 + r * 16, 16), 16), :] = group

                @pl.when(k != hh)
                def _():
                    ns[xi, rows, :] = group


    def norm(r, _):
        norm_chunk(r)
        return 0

    lax.fori_loop(0, 8, norm, 0)
    swap = rdma(
        ns, nb.at[:, pl.ds(pl.multiple_of(k * 128, 128), 128), :], one_s.at[0], one_r.at[0], other
    )
    swap.start()
    drains.append(swap.wait_send)


    def g1_wait(slot, _):
        zi = half * 0 + k * 4 + slot // 2
        mine = jnp.logical_and(zi == z, slot % 2 == k)

        @pl.when(jnp.logical_not(mine))
        def _():
            g1_copy(z, slot).wait_recv()

        return 0

    unrolled(0, 8, g1_wait)
    for xi in range(4):

        @pl.when(x == xi)
        def _():
            tiles = placement(xi)[1]
            columns = [jnp.zeros((16, 128), F32) for _ in range(6)]
            for slot in range(8):
                piece = g1[slot].astype(F32)
                start = (slot // 2 * 672 + xi * 168) % 128 + slot % 2 * ROWS
                m, lead = start // 128, start % 128
                moved = pltpu.roll(piece, lead, 1) if lead else piece
                tile = tiles[slot // 2, m]
                columns[tile] = columns[tile] + jnp.where(lane128 >= lead, moved, 0.0)
                if lead + ROWS > 128:
                    tile = tiles[slot // 2, m + 1]
                    columns[tile] = columns[tile] + jnp.where(lane128 < lead, moved, 0.0)
            own = pl.ds(pl.multiple_of(y * 16, 16), 16)
            wb[xi, parity, own, :] = jnp.concatenate(columns, axis=1).astype(BF16)

    def piece_at(matrix, xi, yi):
        return wb.at[xi, matrix, pl.ds(pl.multiple_of(yi * 16, 16), 16), :]

    def y_copy(src_y, dst_y, t):
        piece = piece_at(parity, x, src_y)
        return rdma(piece, piece, y_s.at[t], y_r.at[src_y], at_y(dst_y))

    def x_copy(src_x, yi, dst_x, t):
        piece = piece_at(parity, src_x, yi)
        return rdma(piece, piece, x_s.at[t, yi], x_r.at[src_x, yi], at_x(dst_x))

    def f_copy(matrix, xi, yi):
        piece = piece_at(matrix, xi, yi)
        target = at_z((z + 1 + 6 * (yi % 2)) % 8, k)
        return rdma(piece, piece, f_s.at[xi, yi], f_r.at[xi, yi], target)

    def y_send(t, _):
        y_copy(y, (y + far_step(t)) % 8, t).start()
        return 0

    unrolled(0, 7, y_send)

    def y_drain(t, _):
        y_copy(y, (y + far_step(t)) % 8, t).wait_send()
        return 0

    drains.append(lambda: unrolled(0, 7, y_drain))

    def x_send(yi):
        for t, dx in enumerate((2, 1, 3)):
            x_copy(x, yi, (x + dx) % 4, t).start()
        f_copy(parity, x, yi).start()

    x_send(y)
    lane = lax.broadcasted_iota(jnp.int32, (128, 128), 1)
    sub = lax.broadcasted_iota(jnp.int32, (128, 128), 0)
    angle = (ctx * 128 + sub).astype(F32) * freq[...]
    cs[0] = jnp.cos(angle)
    cs[1] = jnp.sin(angle) * jnp.where(lane < 64, -1.0, 1.0)
    key_doc = jnp.transpose(jnp.broadcast_to(segb[0, 0:1].astype(F32), (128, 128)))

    def y_forward(t, _):
        src = (y + ring_step(t)) % 8
        y_copy(src, y, 0).wait_recv()
        x_send(src)
        return 0

    unrolled(0, 7, y_forward)

    def x_drain(yi, _):
        for t, dx in enumerate((2, 1, 3)):
            x_copy(x, yi, (x + dx) % 4, t).wait_send()
        for xi in range(4):
            f_copy(parity, xi, yi).wait_send()
        return 0

    drains.append(lambda: unrolled(0, 8, x_drain))

    def x_forward(t, _):
        yi = (y + ring_step(t - 1)) % 8
        for dx in (1, 3, 2):
            xi = (x + dx) % 4
            x_copy(xi, yi, x, 0).wait_recv()
            f_copy(parity, xi, yi).start()
        return 0

    unrolled(0, 8, x_forward)

    for copy in qu_far():
        copy.wait_recv()

    for dx in (2, 1, 3):
        for copy in qu_chip(dx):
            copy.start()
            drains.append(copy.wait_send)
    for copy in qu_core():
        copy.start()
        drains.append(copy.wait_send)

    swap.wait_recv()
    first = jnp.zeros((256, 128), F32)
    for xi in range(4):
        first = first + dot_nt(nb[xi], wb[xi, parity])
    kl[parity] = first
    second = jnp.zeros((256, 128), F32)
    for xi in range(4):

        def f_wait(yi, _):
            f_copy(1 - parity, xi, yi).wait_recv()
            return 0

        unrolled(0, 8, f_wait)
        second = second + dot_nt(nb[xi], wb[xi, 1 - parity])
    kl[1 - parity] = second
    mine = pl.ds(pl.multiple_of(k * 128, 128), 128)
    theirs = pl.ds(pl.multiple_of((1 - k) * 128, 128), 128)
    kl_swap = rdma(kl.at[:, theirs], klr, one_s.at[1], one_r.at[1], other)
    kl_swap.start()
    drains.append(kl_swap.wait_send)
    for dx in (1, 3, 2):
        for copy in qu_chip(dx):
            copy.wait_recv()
        for copy in qu_next(dx):
            copy.start()
            drains.append(copy.wait_send)

    for j in range(1, 8, 2):
        for copy in qu_pair(0, j, other):
            copy.wait_recv()
    kl_swap.wait_recv()
    lin, tan = kl[0, mine] + klr[0], kl[1, mine] + klr[1]
    cosine, sine = cs[0], cs[1]
    key_gain = kg[...]

    def rope(vec):
        return vec * cosine + pltpu.roll(vec, 64, 1) * sine

    def rope_back(vec):
        return vec * cosine - pltpu.roll(vec, 64, 1) * sine

    def mean(vec):
        return jnp.mean(vec, axis=-1, keepdims=True)

    inv = lax.rsqrt(mean(lin * lin) + EPSILON)
    inv3 = inv * inv * inv
    inv_tan = -inv3 * mean(lin * tan)
    keyed = rope(lin * inv * key_gain) * SCORE_SCALE
    keyed_tan = rope((tan * inv + lin * inv_tan) * key_gain) * SCORE_SCALE
    k_high, k_low = split(keyed)
    t_high, t_low = split(keyed_tan)
    stacked_keys = jnp.concatenate([k_high, k_low, t_high, t_low], axis=0)
    value_rows = v_own[...]

    def score(j, _):
        raw = dot_nt(stacked_keys, qu[j, 0])
        s = raw[0:128] + raw[128:256]
        st = raw[256:384] + raw[384:512]
        g = dot_nt(value_rows, qu[j, 1])
        gap = 128 * j + lane - sub
        near = jnp.logical_and(gap >= 0, gap < WINDOW)
        same = key_doc == segb[j, 0:1].astype(F32)
        allowed = jnp.logical_and(jnp.logical_and(near, same), ctx + j < 64)
        top = jnp.max(jnp.where(allowed, s, LOW), axis=0, keepdims=True)
        e = jnp.where(allowed, jnp.exp(s - top), 0.0)
        est = e * st
        rows = [top] + [jnp.sum(m, axis=0, keepdims=True) for m in (e, e * g, est, est * g)]
        rst[8, j] = jnp.concatenate(rows + [jnp.zeros((3, 128), F32)], axis=0)
        ev[j] = e
        sv[j] = st
        gv[j] = g
        return 0

    for j in range(9):
        score(j, 0)

    def st_copies():
        copies = []
        for d in (8, 7, 6, 5, 4, 3, 2, 1):
            n = 9 - d
            copies.append(
                rdma(
                    rst.at[8, pl.ds(d, n)],
                    rst.at[8 + d, pl.ds(0, n)],
                    st_s.at[d - 1],
                    st_r.at[d - 1],
                    at_ctx(ctx + d),
                )
            )
            copies.append(
                rdma(
                    rst.at[8, pl.ds(0, n)],
                    rst.at[8 - d, pl.ds(d, n)],
                    st_s.at[7 + d],
                    st_r.at[7 + d],
                    at_ctx(ctx + 64 - d),
                )
            )
        return copies

    st_list = st_copies()
    for copy in st_list:
        copy.start()
        drains.append(copy.wait_send)
    finish()
    for copy in st_list:
        copy.wait_recv()

    def gradient(j, _):
        stats = [rst[8 - j + t, j] for t in range(9)]
        peak = stats[0][0:1]
        for stat in stats[1:]:
            peak = jnp.maximum(peak, stat[0:1])
        total = jnp.zeros((8, 128), F32)
        for stat in stats:
            total = total + jnp.exp(stat[0:1] - peak) * stat
        filled = total[1:2] > 0.0
        scale = jnp.where(filled, 1.0 / jnp.where(filled, total[1:2], 1.0), 0.0)
        m = total[2:3] * scale
        a = total[3:4] * scale
        m_tan = total[4:5] * scale - a * m
        p = ev[j] * (jnp.exp(rst[8, j][0:1] - peak) * scale)
        rest = gv[j] - m
        ds = p * rest
        ds_tan = p * ((sv[j] - a) * rest - m_tan)
        high, low = split(jnp.concatenate([ds, ds_tan], axis=0))
        prod = dot_nn(jnp.concatenate([high, low], axis=0), qu[j, 0])
        acc[...] += prod[0:256] + prod[256:512]
        return 0

    acc[...] = jnp.zeros((256, 128), F32)
    for j in range(9):
        gradient(j, 0)

    w = rope_back(acc[0:128] * SCORE_SCALE) * key_gain
    w_tan = rope_back(acc[128:256] * SCORE_SCALE) * key_gain
    xw = mean(lin * w)
    xw_tan = mean(tan * w) + mean(lin * w_tan)
    cot = (
        inv_tan * w
        + inv * w_tan
        - tan * (inv3 * xw)
        - lin * (3.0 * inv * inv * inv_tan * xw + inv3 * xw_tan)
    )
    cott[k] = jnp.transpose(cot).astype(BF16)
    cot_swap = rdma(cott.at[k], cott.at[k], one_s.at[2], one_r.at[2], other)
    cot_swap.start()
    drains.append(cot_swap.wait_send)
    cot_in = rdma(cott.at[1 - k], cott.at[1 - k], one_s.at[2], one_r.at[2], other)
    cot_in.wait_recv()
    cots = jnp.concatenate([cott[0], cott[1]], axis=1)

    def slice_of(yi):
        return pl.ds(pl.multiple_of(yi * 16, 16), 16)

    def rx_copy(dx, yi):
        cols = slice_of(yi)
        return rdma(
            ta.at[dx, cols], rx.at[dx - 1, cols], rx_s.at[dx - 1, yi], rx_r.at[dx - 1, yi], at_x((x + dx) % 4)
        )

    def sy_copy(dy):
        yi = (y + dy) % 8
        return rdma(tb.at[:, slice_of(yi)], sy.at[dy], sy_s.at[dy - 1], sy_r.at[dy - 1], at_y(yi))

    for dx in range(4):
        part = dot_nn(cots, nb[(x + dx) % 4, :, CUT:GROUP])
        tb[dx] = part
        if dx == 0:
            py[:, CUT:GROUP] = part

    def sy_send(t, _):
        sy_copy(far_step(t)).start()
        return 0

    unrolled(0, 7, sy_send)
    for dx in (2, 1, 3):
        ta[dx] = dot_nn(cots, nb[(x + dx) % 4, :, 0:CUT])

    def rx_send(t, _):
        for dx in (2, 1, 3):
            rx_copy(dx, (y + far_step(t)) % 8).start()
        return 0

    unrolled(0, 8, rx_send)
    py[:, 0:CUT] = dot_nn(cots, nb[x, :, 0:CUT])

    def rx_drain(yi, _):
        for dx in (2, 1, 3):
            rx_copy(dx, yi).wait_send()
        return 0

    drains.append(lambda: unrolled(0, 8, rx_drain))

    bas[0:6, :, 0:ROWS] = bas_own[...]
    bas[6, :, 0:ROWS] = dir_own[...]
    lane8 = lax.broadcasted_iota(jnp.int32, (8, 128), 1)
    sub8 = lax.broadcasted_iota(jnp.int32, (8, 128), 0)
    gram = jnp.zeros((8, 128), F32)
    for a in range(7):
        for b in range(a, 7):
            dotted = jnp.sum(jnp.sum(bas[a] * bas[b], axis=0, keepdims=True), axis=1, keepdims=True)
            spot = jnp.logical_and(sub8 == a, lane8 == 64 + b)
            if a != b:
                spot = jnp.logical_or(spot, jnp.logical_and(sub8 == b, lane8 == 64 + a))
            gram = jnp.where(spot, dotted, gram)

    def rx_sum(yi):
        cols = slice_of(yi)
        total = py[cols, 0:CUT]
        for dx in (1, 3, 2):
            rx_copy(dx, yi).wait_recv()
            total = total + rx[dx - 1, cols, :]
        return total

    def ry_copy(dy):
        yi = (y + dy) % 8
        return rdma(ta.at[0, slice_of(yi)], ry.at[dy], ry_s.at[dy - 1], ry_r.at[dy - 1], at_y(yi))

    def y_sum(t, _):
        dy = far_step(t)
        yi = (y + dy) % 8
        ta[0, slice_of(yi), :] = rx_sum(yi)
        ry_copy(dy).start()
        return 0

    unrolled(0, 7, y_sum)

    def sy_wait(t, _):
        sy_copy(ring_step(t)).wait_recv()
        return 0

    unrolled(0, 7, sy_wait)

    def sx_copy(dx):
        return rdma(sx.at[dx], sx.at[3 + dx], sx_s.at[dx - 1], sx_r.at[dx - 1], at_x((x + dx) % 4))

    for dx in (2, 1, 3, 0):
        part = tb[dx, slice_of(y), :] if dx else py[slice_of(y), CUT:GROUP]
        for dy in range(1, 8):
            part = part + sy[dy, dx]
        if dx:
            sx[dx] = part
            sx_copy(dx).start()
            drains.append(sx_copy(dx).wait_send)
    total_a = rx_sum(y)

    def ry_wait(t, _):
        ry_copy(ring_step(t)).wait_recv()
        return 0

    unrolled(0, 7, ry_wait)
    for dy in range(1, 8):
        total_a = total_a + ry[dy]
    for dx in (1, 3, 2):
        sx_copy(dx).wait_recv()
        part = part + sx[3 + dx]
    total = jnp.concatenate([total_a, part], axis=1)

    def ry_drain(t, _):
        ry_copy(t + 1).wait_send()
        sy_copy(t + 1).wait_send()
        return 0

    drains.append(lambda: unrolled(0, 7, ry_drain))

    def pz_copy(slot, src_z):
        zi = k * 4 + slot // 2
        return rdma(pz.at[slot], rz.at[src_z], rz_s.at[slot], rz_r.at[src_z], at_z(zi, slot % 2))

    for xi in range(4):

        @pl.when(x == xi)
        def _():
            tiles = placement(xi)[1]
            for slot in range(8):
                start = (slot // 2 * 672 + xi * 168) % 128 + slot % 2 * ROWS
                m, lead = start // 128, start % 128
                tile = tiles[slot // 2, m]
                piece = total[:, tile * 128 : tile * 128 + 128]
                if lead:
                    piece = pltpu.roll(piece, 128 - lead, 1)
                if lead + ROWS > 128:
                    tile = tiles[slot // 2, m + 1]
                    following = pltpu.roll(total[:, tile * 128 : tile * 128 + 128], 128 - lead, 1)
                    piece = jnp.where(lane128 < 128 - lead, piece, following)
                pz[slot] = jnp.where(lane128 < ROWS, piece, 0.0)

    def pz_self(slot):
        return jnp.logical_and(k * 4 + slot // 2 == z, slot % 2 == k)

    def pz_send(t, _):
        slot = (own_slot + 1 + t) % 8

        @pl.when(jnp.logical_not(pz_self(slot)))
        def _():
            pz_copy(slot, z).start()

        @pl.when(pz_self(slot))
        def _():
            rz[z] = pz[slot]

        return 0

    unrolled(0, 8, pz_send)

    def pz_drain(slot, _):
        @pl.when(jnp.logical_not(pz_self(slot)))
        def _():
            pz_copy(slot, z).wait_send()

        return 0

    drains.append(lambda: unrolled(0, 8, pz_drain))

    def rz_wait(t, _):
        src = (z + t) % 8

        @pl.when(jnp.logical_or(src != z, half != k))
        def _():
            pz_copy(0, src).wait_recv()

        return 0

    unrolled(0, 8, rz_wait)
    product = rz[0]
    for src in range(1, 8):
        product = product + rz[src]
    product = product * D ** (-0.5)

    rows = [jnp.sum(bas[a] * product, axis=0, keepdims=True) for a in range(7)]
    rows.append(jnp.sum(product * product, axis=0, keepdims=True))
    sums = jnp.concatenate(rows, axis=0)
    sums = jnp.where(lane8 < 64, sums + pltpu.roll(sums, 64, 1), gram)

    def all_sum(stage, value, own, device):
        ar[stage, own] = value

        def copy(src, t, target):
            return rdma(
                ar.at[stage, src], ar.at[stage, src], ar_s.at[stage, t], ar_r.at[stage, src], device(target)
            )

        def send(t, _):
            copy(own, t, (own + far_step(t)) % 8).start()
            return 0

        unrolled(0, 7, send)
        finish()

        def wait(t, _):
            copy((own + ring_step(t)) % 8, 0, own).wait_recv()
            return 0

        unrolled(0, 7, wait)
        total = ar[stage, 0]
        for i in range(1, 8):
            total = total + ar[stage, i]

        def drain(t, _):
            copy(own, t, (own + far_step(t)) % 8).wait_send()
            return 0

        drains.append(lambda: unrolled(0, 7, drain))
        return total

    sums = all_sum(0, sums, x * 2 + k, lambda i: (z * 8 + i, y))
    sums = all_sum(1, sums, z, lambda i: (i * 8 + x * 2 + k, y))
    sums = all_sum(2, sums, y, lambda i: (ctx, i))
    inner = jnp.sum(jnp.where(lane8 < 64, sums, 0.0), axis=1, keepdims=True)
    coef = jnp.broadcast_to(inner / ENTRIES, (8, 128))
    spots = jnp.logical_and(sub8 == lane8 % 64, sub8 < 7)
    coef_row = jnp.sum(jnp.where(spots, coef, 0.0), axis=0, keepdims=True)
    quad = jnp.sum(jnp.where(lane8 < 64, 0.0, coef_row * sums), axis=1, keepdims=True)
    norm = jnp.where(sub8 < 7, coef * (quad - 2.0 * inner), jnp.broadcast_to(inner, (8, 128)))
    squared = jnp.maximum(jnp.sum(norm, axis=0, keepdims=True), 0.0) / ENTRIES
    beta = jnp.sqrt(squared + EPSILON)
    residual = product
    for a in range(7):
        residual = residual - coef[a : a + 1] * bas[a]
    out[...] = (residual / beta)[:, 0:ROWS]
    coef_out[...] = coef_row[:, 0:7]
    beta_out[...] = beta[:, 0:1]

    finish()


def hand_over(coef_in, beta_in, next_in, coef_out, beta_out, next_out):
    coef_out[...] = coef_in[...]
    beta_out[...] = beta_in[...]
    next_out[...] = next_in[...]


def body(
    tokens,
    norm_gain,
    queries,
    values,
    upstream,
    segments,
    key_weight,
    key_gain,
    direction,
    stored_basis,
):
    dma = pltpu.SemaphoreType.DMA
    vmem = pl.BlockSpec(memory_space=pltpu.VMEM)
    out, coefficients, beta = pl.pallas_call(
        kernel,
        out_shape=tuple(jax.ShapeDtypeStruct(shape, F32) for shape in ((16, ROWS), (1, 7), (1, 1))),
        in_specs=[pl.BlockSpec(memory_space=pl.ANY)] * 11,
        out_specs=(vmem,) * 3,
        scratch_shapes=[
            pltpu.VMEM((128, D), BF16),
            pltpu.VMEM((D // 128, 128), BF16),
            pltpu.VMEM((128, 128), BF16),
            pltpu.VMEM((1, 128), jnp.int32),
            pltpu.VMEM((16, ROWS), BF16),
            pltpu.VMEM((16, ROWS), F32),
            pltpu.VMEM((1, 128), F32),
            pltpu.VMEM((1, 128), F32),
            pltpu.VMEM((6, 16, ROWS), F32),
            pltpu.VMEM((2, 16, 128), BF16),
            pltpu.VMEM((7, 16, 128), F32),
            pltpu.VMEM((8, 16, 128), BF16),
            pltpu.VMEM((4, 2, 128, GROUP), BF16),
            pltpu.VMEM((4, 256, GROUP), BF16),
            pltpu.VMEM((4, 128, GROUP), BF16),
            pltpu.VMEM((9, 2, 128, 128), BF16),
            pltpu.VMEM((9, 8, 128), jnp.int32),
            pltpu.VMEM((2, 256, 128), F32),
            pltpu.VMEM((2, 128, 128), F32),
            pltpu.VMEM((9, 128, 128), F32),
            pltpu.VMEM((9, 128, 128), F32),
            pltpu.VMEM((9, 128, 128), F32),
            pltpu.VMEM((17, 9, 8, 128), F32),
            pltpu.VMEM((2, 128, 128), BF16),
            pltpu.VMEM((256, 128), F32),
            pltpu.VMEM((4, 128, CUT), F32),
            pltpu.VMEM((4, 128, GROUP - CUT), F32),
            pltpu.VMEM((3, 128, CUT), F32),
            pltpu.VMEM((128, GROUP), F32),
            pltpu.VMEM((8, 16, CUT), F32),
            pltpu.VMEM((8, 4, 16, GROUP - CUT), F32),
            pltpu.VMEM((7, 16, GROUP - CUT), F32),
            pltpu.VMEM((8, 16, 128), F32),
            pltpu.VMEM((8, 16, 128), F32),
            pltpu.VMEM((3, 8, 8, 128), F32),
            pltpu.VMEM((2, 128, 128), F32),
            dma((8,)),
            dma((8,)),
            dma((8,)),
            dma((8,)),
            dma((8,)),
            dma((8,)),
            dma((7,)),
            dma((8,)),
            dma((3, 8)),
            dma((4, 8)),
            dma((4, 8)),
            dma((4, 8)),
            dma((3,)),
            dma((3,)),
            dma((11,)),
            dma((16,)),
            dma((16,)),
            dma((3, 8)),
            dma((3, 8)),
            dma((7,)),
            dma((7,)),
            dma((7,)),
            dma((7,)),
            dma((3,)),
            dma((3,)),
            dma((8,)),
            dma((8,)),
            dma((3, 7)),
            dma((3, 8)),
        ],
        compiler_params=pltpu.CompilerParams(
            collective_id=0, has_side_effects=True, vmem_limit_bytes=56 * 2**20
        ),
        name="lanczos_step",
    )(
        tokens[0],
        norm_gain.reshape(D // 128, 128),
        queries[0],
        values[0],
        upstream[0],
        segments,
        key_weight.T,
        direction.T,
        key_gain[None],
        jnp.asarray(FREQS),
        jnp.swapaxes(stored_basis, 1, 2),
    )
    coefficients, beta, out = pl.pallas_call(
        hand_over,
        out_shape=tuple(jax.ShapeDtypeStruct(shape, F32) for shape in ((1, 7), (1, 1), (16, ROWS))),
        in_specs=[vmem] * 3,
        out_specs=(vmem,) * 3,
        name="hand_over",
    )(coefficients, beta, out)
    return coefficients.reshape(7), beta.reshape(()), out.T


def solution(mesh):
    in_specs = (
        P("dp", "ctx", None),
        P(),
        P("dp", "ctx", None),
        P("dp", "ctx", None),
        P("dp", "ctx", None),
        P("dp", "ctx"),
        P("ctx", "dp"),
        P(),
        P("ctx", "dp"),
        P(None, "ctx", "dp"),
    )
    out_specs = (P(), P(), P("ctx", "dp"))
    return jax.shard_map(body, mesh=mesh, in_specs=in_specs, out_specs=out_specs, check_vma=False)
```
